32 devices in a mesh: groups: 2 (over y), dp: 8 (over z, x), tensor: 2 (over core).
Axes of the slice: x: 2, y: 2, z: 4, core: 2. Of those that a mesh axis runs over, the one named last changes fastest.
Arguments:
- inputs: bfloat16 [2048, 8192], P(('groups', 'dp'), 'tensor'), parts along dimension 0, may hold values from -6 to 6
- value_output_gradient: bfloat16 [2048, 1024], P(('groups', 'dp'), 'tensor'), parts along dimension 0, may hold values from -6 to 6
- value_projection_weight: bfloat16 [8192, 1024], P('dp', 'tensor'), may hold values from -0.1875 to 0.1875
- adapter_down_factor: bfloat16 [4, 16, 8192], P(None, None, ('dp', 'tensor')), may hold values from -0.29882812 to 0.29882812
- adapter_up_factor: bfloat16 [4, 16, 1024], P(None, None, 'tensor'), may hold values from -0.1875 to 0.1875
- membership: int32 [4, 16], P(None, ('groups', 'dp')), parts along dimension 1, may hold values from 0 to 1, as said below
- active_token_lengths: int32 [16], P(('groups', 'dp')), parts along dimension 0, may hold values from 1 to 128, 768 in all
Outputs:
- grad_inputs: bfloat16 [2048, 8192], P(('groups', 'dp'), 'tensor'), parts along dimension 0
- grad_down: float32 [2, 8192, 64], P('tensor', ('groups', 'dp')), parts along dimension 1
- grad_up: float32 [2, 1024, 64], P('tensor', ('groups', 'dp')), parts along dimension 1
The draws below stay inside these ranges and needn't reach their ends.
There are 2 independent parts, one for each index of `groups`. The reference program is written for one: setup_inputs(seed, part) draws one part's arguments, and reference() takes and returns one part's arrays. A program takes and returns all parts, laid end to end along the dimension named above; an argument that names none is the same for every part. Nothing has to cross between parts.
Inputs may be any that keep to these rules, and one draw needn't show every extreme that they name: `membership`: each column has exactly one 1; every job owns 8 // 4 micro-batches.
All inputs are finite; a program needn't handle non-finite values. No bound on the sum of `active_token_lengths` on one device may be relied on, other than what follows from the above.
Results may differ from the reference program's by a relative error of at most 0.008.
Values may be sent and summed in bfloat16 or wider, within the bound.
A program may use at most 64 MiB of HBM per device.

```python
import math
import jax
import jax.numpy as jnp
import numpy as np
from jax import lax

MODEL_WIDTH = 8192
VALUE_FEATURES = 1024
ADAPTER_RANK = 16
TENANT_JOBS = 4
TOK_DEV = 128
MICRO = 8
TOKENS = 1024
N_TENSOR = 2


def draw_membership(key, part):
    key = jax.random.fold_in(key, 11)
    order = jax.random.permutation(key, MICRO)
    job_ids = order % TENANT_JOBS
    return (jnp.arange(TENANT_JOBS, dtype=jnp.int32)[:, None] == job_ids[None, :]).astype(jnp.int32)


def level_of(rng, shape, split, low, high):
    def one(axis_at, shards_of):
        steps = jax.random.uniform(jax.random.fold_in(jax.random.fold_in(rng, 6), axis_at), (shards_of,), jnp.float32, low / len(split), high / len(split))
        return jnp.repeat(jnp.exp(steps), shape[axis_at] // shards_of).reshape((-1,) + (1,) * (len(shape) - axis_at - 1))

    factor_of = one(*split[0])
    for cut in split[1:]:
        factor_of = factor_of * one(*cut)
    return factor_of


def profile(amount, total, limit, slope):
    weights = [(1 << 20) // math.isqrt(standing ** slope) + 1 for standing in range(2, amount + 1)]
    rest, counts = total - limit - (amount - 1), [1] * (amount - 1)
    while rest > 0:
        candidates = [i for i in range(amount - 1) if counts[i] < limit]
        mass, remaining = sum([weights[i] for i in candidates]), rest
        for i in candidates:
            more = min(limit - counts[i], max(1, remaining * weights[i] // mass), rest)
            counts[i] = counts[i] + more
            rest = rest - more
    return np.array([limit] + counts)


def ragged(rng, amount, total, bound, lean):
    if amount == 2:
        one = jax.random.randint(rng, (), max(1, total - bound), min(bound, total - 1) + 1)
        return jnp.stack([one, total - one])
    tallies = jnp.asarray(profile(amount, total, bound, lean), jnp.int32)
    twos = (amount - 1) // 2
    giver, taker = tallies[1:1 + 2 * twos:2], tallies[2:2 + 2 * twos:2]
    slack = jnp.minimum(giver - 1, bound - taker)
    passed = jax.random.randint(jax.random.fold_in(rng, 1), (twos,), 0, 1 << 20) % (slack + 1)
    tallies = tallies.at[1:1 + 2 * twos:2].set(giver - passed).at[2:2 + 2 * twos:2].set(taker + passed)
    return tallies[jax.random.permutation(jax.random.fold_in(rng, 2), amount)]


def centred(rng, dims, scale, bound, split=(), held_as=jnp.bfloat16):
    values = scale * jax.random.normal(rng, dims, jnp.float32)
    if split:
        values = values * level_of(rng, dims, split, -0.22, 0.18)
    return jnp.clip(values, -bound, bound).astype(held_as)


def setup_inputs(seed: int = 0, part: int = 0) -> dict:
    streams_of = jax.random.split(jax.random.key(seed), 8)
    part_keys = jax.random.split(jax.random.fold_in(streams_of[7], part), 8)
    inputs = centred(part_keys[0], (TOKENS, MODEL_WIDTH), 1.0, 6.0, ((0, 8), (1, 2)))
    value_output_gradient = centred(part_keys[1], (TOKENS, VALUE_FEATURES), 1.0, 6.0, ((0, 8), (1, 2)))
    value_projection_weight = centred(streams_of[2], (MODEL_WIDTH, VALUE_FEATURES), VALUE_FEATURES ** -0.5, 0.1875, ((0, 8), (1, 2)))
    adapter_down_factor = centred(streams_of[3], (TENANT_JOBS, ADAPTER_RANK, MODEL_WIDTH), 0.05, 0.29882812, ((2, 16),))
    adapter_up_factor = centred(streams_of[4], (TENANT_JOBS, ADAPTER_RANK, VALUE_FEATURES), VALUE_FEATURES ** -0.5, 0.1875, ((2, 2),))
    membership = draw_membership(jax.random.fold_in(jax.random.fold_in(streams_of[7], part), 71), part)
    active_token_lengths = ragged(part_keys[6], MICRO, MICRO * TOK_DEV * 3 // 4, TOK_DEV, 2).astype(jnp.int32)
    return {"inputs": inputs, "value_output_gradient": value_output_gradient, "value_projection_weight": value_projection_weight, "adapter_down_factor": adapter_down_factor, "adapter_up_factor": adapter_up_factor, "membership": membership, "active_token_lengths": active_token_lengths}


adapter_scale = 2.0


def reference(inputs, value_output_gradient, value_projection_weight, adapter_down_factor, adapter_up_factor, membership, active_token_lengths):
    head_half = VALUE_FEATURES // N_TENSOR
    live_all = jnp.arange(TOK_DEV, dtype=jnp.int32)[None, :] < active_token_lengths[:, None]
    input_blocks = inputs.reshape(MICRO, TOK_DEV, MODEL_WIDTH)
    grad_blocks = value_output_gradient.reshape(MICRO, TOK_DEV, VALUE_FEATURES)
    job_rows = membership.T
    broad_down_factor = adapter_down_factor.astype(jnp.float32)
    broad_up_factor = adapter_up_factor.astype(jnp.float32)

    def one_block(carry, item):
        sum_down, sum_up = carry
        x_block, g_block, live_rows, own_row = item
        grad_masked = jnp.where(live_rows[:, None], g_block, jnp.zeros_like(g_block))
        own_float = own_row.astype(jnp.float32)
        job_down_factor = jnp.einsum("j,jrd->rd", own_float, broad_down_factor).astype(jnp.bfloat16)
        up_job = jnp.einsum("p,pxh->xh", own_float, broad_up_factor).astype(jnp.bfloat16)
        fixed_weight = jnp.zeros((TOK_DEV, MODEL_WIDTH), jnp.float32)
        for shard_idx in range(N_TENSOR):
            cols = slice(shard_idx * head_half, (shard_idx + 1) * head_half)
            group_sum = jnp.dot(grad_masked[:, cols], value_projection_weight[:, cols].T, preferred_element_type=jnp.float32)
            rounded = lax.optimization_barrier(group_sum.astype(jnp.bfloat16))
            fixed_weight = fixed_weight + rounded.astype(jnp.float32)
        projected = jnp.dot(x_block, job_down_factor.T, preferred_element_type=jnp.float32)
        projected = jnp.where(live_rows[:, None], projected, jnp.zeros_like(projected)).astype(jnp.bfloat16)
        rank_gradient_back = jnp.dot(grad_masked, up_job.T, preferred_element_type=jnp.float32).astype(jnp.bfloat16)
        gradient_tile_block = (fixed_weight + adapter_scale * jnp.dot(rank_gradient_back, job_down_factor, preferred_element_type=jnp.float32)).astype(jnp.bfloat16)
        term_down = jnp.dot(x_block.T, rank_gradient_back, preferred_element_type=jnp.float32)
        term_up = jnp.dot(grad_masked.T, projected, preferred_element_type=jnp.float32)
        sum_down = sum_down + own_float[None, :, None] * term_down[:, None, :]
        sum_up = sum_up + own_float[None, :, None] * term_up[:, None, :]
        return (sum_down, sum_up), gradient_tile_block

    start_carry = (jnp.zeros((MODEL_WIDTH, TENANT_JOBS, ADAPTER_RANK), jnp.float32), jnp.zeros((VALUE_FEATURES, TENANT_JOBS, ADAPTER_RANK), jnp.float32))
    (sum_down, sum_up), grad_blocks_out = lax.scan(one_block, start_carry, (input_blocks, grad_blocks, live_all, job_rows))
    tenant_token_rows = jnp.sum(membership.astype(jnp.float32) * active_token_lengths.astype(jnp.float32)[None, :], axis=1)
    factor_matrix = adapter_scale / tenant_token_rows
    grad_down = (sum_down * factor_matrix[None, :, None]).reshape(N_TENSOR, MODEL_WIDTH // N_TENSOR, TENANT_JOBS * ADAPTER_RANK)
    grad_up = (sum_up * factor_matrix[None, :, None]).reshape(N_TENSOR, VALUE_FEATURES // N_TENSOR, TENANT_JOBS * ADAPTER_RANK)
    return grad_blocks_out.reshape(TOKENS, MODEL_WIDTH), grad_down, grad_up
```

```python
import functools

import jax
import jax.numpy as jnp
from jax import lax
from jax.experimental import pallas as pl
from jax.experimental.pallas import tpu as pltpu
from jax.sharding import PartitionSpec as P

adapter_scale = 2.0
MESH = pl.DeviceIdType.MESH


def contract_rows(left, right):
    return lax.dot_general(
        left, right, (((0,), (0,)), ((), ())), preferred_element_type=jnp.float32
    )


def contract_cols(left, right):
    return lax.dot_general(
        left, right, (((1,), (1,)), ((), ())), preferred_element_type=jnp.float32
    )


def plain_dot(left, right):
    return jnp.dot(left, right, preferred_element_type=jnp.float32)


def wide(row, lanes):
    return jnp.concatenate([row] * (lanes // row.shape[1]), axis=1)


def exchange_kernel(
    dp,
    jobs,
    rank,
    x_ref,
    g_ref,
    w_ref,
    down_ref,
    up_ref,
    meta_ref,
    out_ref,
    gd_ref,
    gu_ref,
    grads,
    w_sib,
    up_sib,
    meta,
    down_out,
    down_in,
    out_buf,
    part_out,
    part_in,
    proj_half,
    proj,
    meta_s, meta_r, g_s, g_r, f_s, f_r, gf_s, gf_r, one_s, one_r,
    d_s, d_r, o_s, o_r, p_s, p_r, j_s, j_r,
):
    tok, heads = g_ref.shape
    feats = down_ref.shape[1]
    cols = jobs * rank
    gi, me, core = lax.axis_index("groups"), lax.axis_index("dp"), lax.axis_index("tensor")
    other = 1 - core
    depth = dp // 2
    z, x = me // 2, me % 2
    owner_core = me // depth
    slot = (2 * me + core) % dp
    ahead = [lax.rem(me + s, dp) for s in range(dp)]

    def remote(src, dst, send, recv, to_dp, to_core):
        return pltpu.make_async_remote_copy(
            src_ref=src, dst_ref=dst, send_sem=send, recv_sem=recv,
            device_id=(gi, to_dp, to_core), device_id_type=MESH,
        )

    length = meta_ref[jobs:jobs + 1, :]
    live = lax.broadcasted_iota(jnp.int32, (tok, heads), 0) < wide(length, heads)
    grads[me, core] = jnp.where(live, g_ref[...], jnp.zeros_like(g_ref))
    meta[me] = meta_ref[...]

    barrier = pltpu.get_barrier_semaphore()
    for s in range(dp):
        for c in range(2):
            if s == 0 and c == 1:
                continue
            to_core = other if s == 0 else c
            pl.semaphore_signal(
                barrier, inc=1, device_id=(gi, ahead[s], to_core), device_id_type=MESH
            )
    pl.semaphore_wait(barrier, 2 * dp - 1)

    sent = []

    def go(copy):
        copy.start()
        sent.append(copy)

    own = grads.at[me, core]
    go(remote(own, own, gf_s.at[me], gf_r.at[me], me, other))
    go(remote(up_ref, up_sib, one_s.at[0], one_r.at[0], me, other))
    for dz in range(1, depth):
        to = lax.rem(z + dz, depth) * 2 + x
        go(remote(own, own, g_s.at[to], g_r.at[me], to, core))
    beside = z * 2 + (1 - x)
    go(remote(own, own, g_s.at[beside], g_r.at[me], beside, core))
    for s in range(1, dp):
        go(remote(meta.at[me], meta.at[me], meta_s.at[ahead[s]], meta_r.at[me], ahead[s], core))
    w_half = w_ref.at[pl.ds(pl.multiple_of(other * feats, feats), feats), :]
    go(remote(w_half, w_sib, one_s.at[1], one_r.at[1], me, other))

    def got(dst, recv):
        remote(dst, dst, one_s.at[0], recv, me, other).wait_recv()

    def pick(rows, b):
        n = rows.shape[1]
        total = jnp.zeros((rank, n), jnp.float32)
        for j in range(jobs):
            held = meta[b, j:j + 1, :].astype(jnp.float32)
            total = total + rows[j * rank:(j + 1) * rank, :].astype(jnp.float32) * wide(held, n)
        return total.astype(jnp.bfloat16)

    got(up_sib, one_r.at[0])
    got(grads.at[me, other], gf_r.at[me])
    up_own, up_other = up_ref[...], up_sib[...]
    back = contract_cols(pick(up_own, me), grads[me, core]) + contract_cols(
        pick(up_other, me), grads[me, other]
    )
    back = back.astype(jnp.bfloat16)
    for b in range(dp):
        part_out[b] = plain_dot(back, x_ref[:, b * feats:(b + 1) * feats]).astype(jnp.bfloat16)
    part_in[me] = part_out[me]
    for s in range(1, dp):
        got(meta.at[ahead[s]], meta_r.at[ahead[s]])
    down_all = down_ref[...]
    for b in range(dp):
        down_out[b] = pick(down_all, b)

    mine = owner_core == core

    def to_owner(src, dst, send, recv, b):
        @pl.when(jnp.logical_and(b == me, mine))
        def _():
            pltpu.make_async_copy(src, dst, recv).start()

        @pl.when(jnp.logical_not(jnp.logical_and(b == me, mine)))
        def _():
            remote(src, dst, send, recv, b, owner_core).start()

    def to_owner_done(src, dst, send, recv, b):
        @pl.when(jnp.logical_not(jnp.logical_and(b == me, mine)))
        def _():
            remote(src, dst, send, recv, b, owner_core).wait_send()

    for s in range(dp):
        b = ahead[s]
        to_owner(down_out.at[b], down_in.at[slot], d_s.at[b], d_r.at[slot], b)
    for s in range(1, dp):
        b = ahead[s]
        go(remote(part_out.at[b], part_in.at[me], p_s.at[b], p_r.at[me], b, core))

    got(w_sib, one_r.at[1])
    w_own = w_ref.at[pl.ds(pl.multiple_of(core * feats, feats), feats), :]
    out_cols = pl.ds(pl.multiple_of(slot * feats, feats), feats)

    def arrive(dz, dx):
        b = lax.rem(z + dz, depth) * 2 + (x if dx == 0 else 1 - x)
        if dz == 0 and dx == 0:
            return b
        block = grads.at[b, core]
        got(block, g_r.at[b])
        go(remote(block, block, gf_s.at[b], gf_r.at[b], me, other))
        if dx == 0:
            go(remote(block, block, f_s.at[b], g_r.at[b], beside, core))
        return b

    def block_out(b, wait_half):
        if wait_half:
            got(grads.at[b, other], gf_r.at[b])
        g_own, g_other = grads[b, core], grads[b, other]
        frozen = contract_cols(g_own, w_own[...]) + contract_cols(g_other, w_sib[...])
        rb = contract_cols(g_own, up_own) + contract_cols(g_other, up_other)
        held = meta[b, jobs + 1:jobs + 2, :cols].astype(jnp.float32)
        rb = (rb.astype(jnp.bfloat16).astype(jnp.float32) * held).astype(jnp.bfloat16)
        out_buf[b] = (frozen + adapter_scale * plain_dot(rb, down_all)).astype(jnp.bfloat16)
        to_owner(out_buf.at[b], out_ref.at[:, out_cols], o_s.at[b], o_r.at[slot], b)

    order = [(dz, 0) for dz in range(1, depth)] + [(0, 1)]
    order += [(dz, 1) for dz in range(1, depth)] + [(0, 0)]
    held_b = arrive(*order[0])
    for i in range(dp):
        later = arrive(*order[i + 1]) if i + 1 < dp else None
        block_out(held_b, order[i] != (0, 0))
        held_b = later
        if i == depth - 1:
            total = jnp.zeros((rank, tok), jnp.float32)
            for k in range(dp):
                got(down_in.at[k], d_r.at[k])
                total = total + contract_cols(down_in[k], x_ref[:, k * feats:(k + 1) * feats])
            proj_half[core] = total
            half = proj_half.at[core]
            go(remote(half, half, one_s.at[2], one_r.at[2], me, other))
        if i == depth:
            got(proj_half.at[other], one_r.at[2])
            full = proj_half[0] + proj_half[1]
            alive = lax.broadcasted_iota(jnp.int32, (rank, tok), 1) < length
            proj[me] = jnp.where(alive, full, jnp.zeros_like(full)).astype(jnp.bfloat16)
            for s in range(1, dp):
                go(remote(proj.at[me], proj.at[me], j_s.at[ahead[s]], j_r.at[me], ahead[s], core))

    tokens = jnp.zeros((1, 128), jnp.float32)
    for b in range(dp):
        tokens = tokens + (meta[b, jobs + 1:jobs + 2, :] * meta[b, jobs:jobs + 1, :]).astype(jnp.float32)
    factor = adapter_scale / tokens[:, :cols]

    for s in range(1, dp):
        got(part_in.at[ahead[s]], p_r.at[ahead[s]])
    same = (
        lax.broadcasted_iota(jnp.int32, (rank, 128), 1) % rank
        == lax.broadcasted_iota(jnp.int32, (rank, 128), 0)
    ).astype(jnp.float32)
    total = jnp.zeros((feats, 128), jnp.float32)
    for b in range(dp):
        place = (same * meta[b, jobs + 1:jobs + 2, :].astype(jnp.float32)).astype(jnp.bfloat16)
        total = total + contract_rows(part_in[b], place)
    gd_ref[...] = total[:, :cols] * factor

    up_rows = heads // dp
    first = pl.multiple_of((me * up_rows) // 128 * 128, 128)
    total = jnp.zeros((128, cols), jnp.float32)
    for s in range(dp):
        b = ahead[s]
        if s:
            got(proj.at[b], j_r.at[b])
        p_b = proj[b].astype(jnp.float32)
        spread = jnp.concatenate(
            [p_b * meta[b, j:j + 1, :].astype(jnp.float32) for j in range(jobs)], axis=0
        ).astype(jnp.bfloat16)
        g_b = grads[b, core, :, pl.ds(first, 128)]
        total = total + lax.dot_general(
            g_b, spread, (((0,), (1,)), ((), ())), preferred_element_type=jnp.float32
        )
    total = total * factor
    picked = total[:up_rows]
    for q in range(1, 128 // up_rows):
        picked = jnp.where(me % (128 // up_rows) == q, total[q * up_rows:(q + 1) * up_rows], picked)
    gu_ref[...] = picked

    for k in range(dp):
        got(out_ref.at[:, k * feats:(k + 1) * feats], o_r.at[k])
    for s in range(dp):
        b = ahead[s]
        to_owner_done(down_out.at[b], down_in.at[slot], d_s.at[b], d_r.at[slot], b)
        to_owner_done(out_buf.at[b], out_ref.at[:, out_cols], o_s.at[b], o_r.at[slot], b)
    for copy in sent:
        copy.wait_send()


def token_body(
    dp,
    inputs,
    value_output_gradient,
    value_projection_weight,
    adapter_down_factor,
    adapter_up_factor,
    membership,
    active_token_lengths,
):
    tok, heads = value_output_gradient.shape
    jobs, rank, feats = adapter_down_factor.shape
    cols = jobs * rank
    own = membership[:, :1]
    meta = jnp.concatenate(
        [
            jnp.broadcast_to(own, (jobs, 128)),
            jnp.broadcast_to(active_token_lengths[:, None], (1, 128)),
            jnp.pad(jnp.repeat(own.T, rank, axis=1), ((0, 0), (0, 128 - cols))),
            jnp.zeros((8 - jobs - 2, 128), jnp.int32),
        ],
        axis=0,
    )
    bf16, f32 = jnp.bfloat16, jnp.float32
    vmem = pl.BlockSpec(memory_space=pltpu.VMEM)
    dma = pltpu.SemaphoreType.DMA
    out, gd, gu = pl.pallas_call(
        functools.partial(exchange_kernel, dp, jobs, rank),
        out_shape=(
            jax.ShapeDtypeStruct((tok, dp * feats), bf16),
            jax.ShapeDtypeStruct((feats, cols), f32),
            jax.ShapeDtypeStruct((heads // dp, cols), f32),
        ),
        in_specs=[vmem] * 6,
        out_specs=(pl.BlockSpec(memory_space=pl.ANY), vmem, vmem),
        scratch_shapes=[
            pltpu.VMEM((dp, 2, tok, heads), bf16),
            pltpu.VMEM((feats, heads), bf16),
            pltpu.VMEM((cols, heads), bf16),
            pltpu.VMEM((dp, 8, 128), jnp.int32),
            pltpu.VMEM((dp, rank, feats), bf16),
            pltpu.VMEM((dp, rank, feats), bf16),
            pltpu.VMEM((dp, tok, feats), bf16),
            pltpu.VMEM((dp, rank, feats), bf16),
            pltpu.VMEM((dp, rank, feats), bf16),
            pltpu.VMEM((2, rank, tok), f32),
            pltpu.VMEM((dp, rank, tok), bf16),
        ]
        + [dma((dp,))] * 8
        + [dma((3,))] * 2
        + [dma((dp,))] * 8,
        compiler_params=pltpu.CompilerParams(
            collective_id=0, has_side_effects=True, vmem_limit_bytes=32 * 2**20
        ),
        cost_estimate=pl.CostEstimate(
            flops=2 * dp * tok * 2 * heads * feats, bytes_accessed=2**23, transcendentals=0
        ),
    )(
        inputs,
        value_output_gradient,
        value_projection_weight,
        adapter_down_factor.reshape(cols, feats),
        adapter_up_factor.reshape(cols, heads),
        meta,
    )
    return out, gd[None], gu[None]


def weight_body(
    inputs,
    value_output_gradient,
    value_projection_weight,
    adapter_down_factor,
    adapter_up_factor,
    membership,
    active_token_lengths,
):
    tok_rows = inputs.shape[0]
    feat_half = inputs.shape[1]
    job_count = membership.shape[0]
    rank_dimension_size = adapter_down_factor.shape[1]
    live_rows = lax.iota(jnp.int32, tok_rows) < active_token_lengths[0]
    grad_masked = jnp.where(
        live_rows[:, None], value_output_gradient, jnp.zeros_like(value_output_gradient)
    )
    own_jobs = membership[:, 0]
    owned_weight_rows = own_jobs.astype(jnp.bfloat16)
    tenant_token_rows = lax.psum(
        own_jobs.astype(jnp.float32) * active_token_lengths[0].astype(jnp.float32), "dp"
    )
    every_down_factor = lax.all_gather(adapter_down_factor, ("dp", "tensor"), axis=2, tiled=True)
    job_down_factor = jnp.einsum(
        "j,jrd->rd", owned_weight_rows, every_down_factor, preferred_element_type=jnp.float32
    ).astype(jnp.bfloat16)
    up_job = jnp.einsum(
        "p,pxh->xh", owned_weight_rows, adapter_up_factor, preferred_element_type=jnp.float32
    ).astype(jnp.bfloat16)
    resident_down_factor = lax.dynamic_slice_in_dim(
        job_down_factor, lax.axis_index("tensor") * feat_half, feat_half, 1
    )
    down_terms = contract_cols(inputs, resident_down_factor)
    up_terms = contract_cols(grad_masked, up_job)
    projected_full, back_full = lax.psum((down_terms, up_terms), "tensor")
    projected = jnp.where(
        live_rows[:, None], projected_full, jnp.zeros_like(projected_full)
    ).astype(jnp.bfloat16)
    rank_gradient_back = back_full.astype(jnp.bfloat16)
    frozen_terms = contract_cols(
        grad_masked, lax.all_gather(value_projection_weight, "dp", axis=0, tiled=True)
    )
    fixed_weight = lax.psum_scatter(
        frozen_terms.astype(jnp.bfloat16), "tensor", scatter_dimension=1, tiled=True
    ).astype(jnp.float32)
    grad_inputs = (
        fixed_weight
        + adapter_scale
        * jnp.dot(rank_gradient_back, resident_down_factor, preferred_element_type=jnp.float32)
    ).astype(jnp.bfloat16)
    wide_cols = job_count * rank_dimension_size
    factor_column_count = jnp.repeat(adapter_scale / tenant_token_rows, rank_dimension_size)
    back_expand = (rank_gradient_back[:, None, :] * owned_weight_rows[None, :, None]).reshape(
        tok_rows, wide_cols
    )
    columns = inputs
    down_sums = lax.psum_scatter(
        contract_rows(columns, back_expand), "dp", scatter_dimension=0, tiled=True
    )
    proj_expand = (projected[:, None, :] * owned_weight_rows[None, :, None]).reshape(
        tok_rows, wide_cols
    )
    columns = grad_masked
    up_sums = lax.psum_scatter(
        contract_rows(columns, proj_expand), "dp", scatter_dimension=0, tiled=True
    )
    grad_down = (down_sums * factor_column_count[None, :])[None]
    grad_up = (up_sums * factor_column_count[None, :])[None]
    return (grad_inputs, grad_down, grad_up)


def solution(mesh):
    in_specs = (
        P(("groups", "dp"), "tensor"),
        P(("groups", "dp"), "tensor"),
        P("dp", "tensor"),
        P(None, None, ("dp", "tensor")),
        P(None, None, "tensor"),
        P(None, ("groups", "dp")),
        P(("groups", "dp")),
    )
    out_specs = (
        P(("groups", "dp"), "tensor"),
        P("tensor", ("groups", "dp"), None),
        P("tensor", ("groups", "dp"), None),
    )

    def body(*args):
        dp = mesh.shape["dp"]
        tok, heads = args[1].shape
        jobs, rank, feats = args[3].shape
        tokens_travel = (
            args[2].shape[0] > tok
            and mesh.shape["tensor"] == 2
            and dp % 2 == 0
            and args[2].shape[0] == 2 * feats
            and tok == 128
            and rank == 16
            and jobs * rank <= 128
            and jobs <= 6
            and feats % 128 == 0
            and heads % (8 * dp) == 0
            and 128 % (heads // dp) == 0
        )
        if tokens_travel:
            return token_body(dp, *args)
        return weight_body(*args)

    return jax.shard_map(body, mesh=mesh, in_specs=in_specs, out_specs=out_specs, check_vma=False)
```

```python
import functools

import jax
import jax.numpy as jnp
from jax import lax
from jax.experimental import pallas as pl
from jax.experimental.pallas import tpu as pltpu
from jax.sharding import PartitionSpec as P

adapter_scale = 2.0
MESH = pl.DeviceIdType.MESH


def contract_rows(left, right):
    return lax.dot_general(
        left, right, (((0,), (0,)), ((), ())), preferred_element_type=jnp.float32
    )


def contract_cols(left, right):
    return lax.dot_general(
        left, right, (((1,), (1,)), ((), ())), preferred_element_type=jnp.float32
    )


def plain_dot(left, right):
    return jnp.dot(left, right, preferred_element_type=jnp.float32)


def wide(row, lanes):
    return jnp.concatenate([row] * (lanes // row.shape[1]), axis=1)


def exchange_kernel(
    dp,
    jobs,
    rank,
    x_hbm,
    g_hbm,
    w_hbm,
    down_hbm,
    up_hbm,
    member_ref,
    length_ref,
    out_ref,
    gd_ref,
    gu_ref,
    x_ref, g_ref, w_ref, down_ref, up_ref,
    grads,
    w_sib,
    up_sib,
    meta,
    down_out,
    down_in,
    out_buf,
    part_out,
    part_in,
    proj_half,
    proj,
    load_s, meta_s, meta_r, g_s, g_r, f_s, zf_s, gf_s, gf_r, one_s, one_r,
    d_s, d_r, o_s, o_r, p_s, p_r, j_s, j_r,
):
    tok, heads = g_ref.shape
    feats = down_ref.shape[1]
    cols = jobs * rank
    gi, me, core = lax.axis_index("groups"), lax.axis_index("dp"), lax.axis_index("tensor")
    other = 1 - core
    depth = dp // 2
    z, x = me // 2, me % 2
    owner_core = me // depth
    slot = (2 * me + core) % dp
    ahead = [lax.rem(me + s, dp) for s in range(dp)]

    def remote(src, dst, send, recv, to_dp, to_core):
        return pltpu.make_async_remote_copy(
            src_ref=src, dst_ref=dst, send_sem=send, recv_sem=recv,
            device_id=(gi, to_dp, to_core), device_id_type=MESH,
        )

    loads = [
        pltpu.make_async_copy(src, dst, load_s.at[i])
        for i, (src, dst) in enumerate(
            [(g_hbm, g_ref), (up_hbm, up_ref), (down_hbm, down_ref), (w_hbm, w_ref), (x_hbm, x_ref)]
        )
    ]
    for load in loads:
        load.start()

    barrier = pltpu.get_barrier_semaphore()
    for s in range(dp):
        for c in range(2):
            if s == 0 and c == 1:
                continue
            to_core = other if s == 0 else c
            pl.semaphore_signal(
                barrier, inc=1, device_id=(gi, ahead[s], to_core), device_id_type=MESH
            )

    row = lax.broadcasted_iota(jnp.int32, (8, 128), 0)
    column = lax.broadcasted_iota(jnp.int32, (8, 128), 1)
    marks = (row == jobs).astype(jnp.int32) * length_ref[0]
    for j in range(jobs):
        by_column = jnp.logical_and(row == jobs + 1, column // rank == j)
        marks = marks + jnp.logical_or(row == j, by_column).astype(jnp.int32) * member_ref[j]
    meta[me] = marks
    length = meta[me, jobs:jobs + 1, :]
    live = lax.broadcasted_iota(jnp.int32, (tok, heads), 0) < wide(length, heads)
    loads[0].wait()
    grads[me, core] = jnp.where(live, g_ref[...], jnp.zeros_like(g_ref))
    loads[1].wait()
    pl.semaphore_wait(barrier, 2 * dp - 1)

    sent = []

    def go(copy):
        copy.start()
        sent.append(copy)

    pair, inner_far, end_far = z ^ 1, jnp.where(z < depth // 2, 2, 1), jnp.where(z < depth // 2, 3, 0)
    is_inner = jnp.logical_or(z == 1, z == 2)
    beside, paired = z * 2 + (1 - x), pair * 2 + x
    own = grads.at[me, core]
    go(remote(own, own, gf_s.at[me], gf_r.at[me], me, other))
    go(remote(up_ref, up_sib, one_s.at[0], one_r.at[0], me, other))
    for s in range(1, dp):
        go(remote(meta.at[me], meta.at[me], meta_s.at[ahead[s]], meta_r.at[me], ahead[s], core))
    for to in (inner_far * 2 + x, paired, beside):
        go(remote(own, own, g_s.at[to], g_r.at[me], to, core))
    loads[3].wait()
    w_half = w_ref.at[pl.ds(pl.multiple_of(other * feats, feats), feats), :]
    go(remote(w_half, w_sib, one_s.at[1], one_r.at[1], me, other))

    def got(dst, recv):
        remote(dst, dst, one_s.at[0], recv, me, other).wait_recv()

    def pick(rows, b):
        n = rows.shape[1]
        total = jnp.zeros((rank, n), jnp.float32)
        for j in range(jobs):
            held = meta[b, j:j + 1, :].astype(jnp.float32)
            total = total + rows[j * rank:(j + 1) * rank, :].astype(jnp.float32) * wide(held, n)
        return total.astype(jnp.bfloat16)

    got(up_sib, one_r.at[0])
    got(grads.at[me, other], gf_r.at[me])
    up_own, up_other = up_ref[...], up_sib[...]
    back = contract_cols(pick(up_own, me), grads[me, core]) + contract_cols(
        pick(up_other, me), grads[me, other]
    )
    back = back.astype(jnp.bfloat16)
    loads[4].wait()
    for b in range(dp):
        part_out[b] = plain_dot(back, x_ref[:, b * feats:(b + 1) * feats]).astype(jnp.bfloat16)
    part_in[me] = part_out[me]
    for s in range(1, dp):
        got(meta.at[ahead[s]], meta_r.at[ahead[s]])
    loads[2].wait()
    down_all = down_ref[...]
    for b in range(dp):
        down_out[b] = pick(down_all, b)

    mine = owner_core == core

    def to_owner(src, dst, send, recv, b):
        @pl.when(jnp.logical_and(b == me, mine))
        def _():
            pltpu.make_async_copy(src, dst, recv).start()

        @pl.when(jnp.logical_not(jnp.logical_and(b == me, mine)))
        def _():
            remote(src, dst, send, recv, b, owner_core).start()

    def to_owner_done(src, dst, send, recv, b):
        @pl.when(jnp.logical_not(jnp.logical_and(b == me, mine)))
        def _():
            remote(src, dst, send, recv, b, owner_core).wait_send()

    for s in range(dp):
        b = ahead[s]
        to_owner(down_out.at[b], down_in.at[slot], d_s.at[b], d_r.at[slot], b)
    for s in range(1, dp):
        b = ahead[s]
        go(remote(part_out.at[b], part_in.at[me], p_s.at[b], p_r.at[me], b, core))

    got(w_sib, one_r.at[1])
    w_own = w_ref.at[pl.ds(pl.multiple_of(core * feats, feats), feats), :]
    out_cols = pl.ds(pl.multiple_of(slot * feats, feats), feats)

    far = []

    def arrive(zs, dx, direct=False):
        b = zs * 2 + (x if dx == 0 else 1 - x)
        block = grads.at[b, core]
        got(block, g_r.at[b])
        if direct:
            copy = remote(block, block, zf_s.at[b], g_r.at[b], paired, core)
            pl.when(is_inner)(copy.start)
            far.append(copy)
        go(remote(block, block, gf_s.at[b], gf_r.at[b], me, other))
        if dx == 0:
            go(remote(block, block, f_s.at[b], g_r.at[b], beside, core))
        return b

    def block_out(b, wait_half):
        if wait_half:
            got(grads.at[b, other], gf_r.at[b])
        g_own, g_other = grads[b, core], grads[b, other]
        frozen = contract_cols(g_own, w_own[...]) + contract_cols(g_other, w_sib[...])
        rb = contract_cols(g_own, up_own) + contract_cols(g_other, up_other)
        held = meta[b, jobs + 1:jobs + 2, :cols].astype(jnp.float32)
        rb = (rb.astype(jnp.bfloat16).astype(jnp.float32) * held).astype(jnp.bfloat16)
        out_buf[b] = (frozen + adapter_scale * plain_dot(rb, down_all)).astype(jnp.bfloat16)
        to_owner(out_buf.at[b], out_ref.at[:, out_cols], o_s.at[b], o_r.at[slot], b)

    order = [
        (inner_far, 0, True), (pair, 0), (end_far, 0, True), (z, 1),
        (inner_far, 1), (pair, 1), (end_far, 1), None,
    ]
    held_b = arrive(*order[0])
    for i in range(dp):
        later = me
        if i + 1 < dp and order[i + 1] is not None:
            later = arrive(*order[i + 1])
        block_out(held_b, order[i] is not None)
        held_b = later
        if i == depth - 1:
            total = jnp.zeros((rank, tok), jnp.float32)
            for k in range(dp):
                got(down_in.at[k], d_r.at[k])
                total = total + contract_cols(down_in[k], x_ref[:, k * feats:(k + 1) * feats])
            proj_half[core] = total
            half = proj_half.at[core]
            go(remote(half, half, one_s.at[2], one_r.at[2], me, other))
        if i == depth:
            got(proj_half.at[other], one_r.at[2])
            full = proj_half[0] + proj_half[1]
            alive = lax.broadcasted_iota(jnp.int32, (rank, tok), 1) < length
            proj[me] = jnp.where(alive, full, jnp.zeros_like(full)).astype(jnp.bfloat16)
            for s in range(1, dp):
                go(remote(proj.at[me], proj.at[me], j_s.at[ahead[s]], j_r.at[me], ahead[s], core))

    tokens = jnp.zeros((1, 128), jnp.float32)
    for b in range(dp):
        tokens = tokens + (meta[b, jobs + 1:jobs + 2, :] * meta[b, jobs:jobs + 1, :]).astype(jnp.float32)
    factor = adapter_scale / tokens[:, :cols]

    for s in range(1, dp):
        got(part_in.at[ahead[s]], p_r.at[ahead[s]])
    same = (
        lax.broadcasted_iota(jnp.int32, (rank, 128), 1) % rank
        == lax.broadcasted_iota(jnp.int32, (rank, 128), 0)
    ).astype(jnp.float32)
    place = jnp.concatenate(
        [same * meta[b, jobs + 1:jobs + 2, :].astype(jnp.float32) for b in range(dp)], axis=0
    ).astype(jnp.bfloat16)
    parts = part_in[...].reshape(dp * rank, feats)
    sums = contract_rows(place, parts)
    for j in range(jobs):
        held = jnp.zeros((1, 128), jnp.float32)
        for b in range(dp):
            held = held + (meta[b, j:j + 1, :] * meta[b, jobs:jobs + 1, :]).astype(jnp.float32)
        gd_ref[j * rank:(j + 1) * rank, :] = sums[j * rank:(j + 1) * rank, :] * wide(
            adapter_scale / held, feats
        )

    up_rows = heads // dp
    first = pl.multiple_of((me * up_rows) // 128 * 128, 128)
    total = jnp.zeros((128, cols), jnp.float32)
    for s in range(dp):
        b = ahead[s]
        if s:
            got(proj.at[b], j_r.at[b])
        p_b = proj[b].astype(jnp.float32)
        spread = jnp.concatenate(
            [p_b * meta[b, j:j + 1, :].astype(jnp.float32) for j in range(jobs)], axis=0
        ).astype(jnp.bfloat16)
        g_b = grads[b, core, :, pl.ds(first, 128)]
        total = total + lax.dot_general(
            g_b, spread, (((0,), (1,)), ((), ())), preferred_element_type=jnp.float32
        )
    total = total * factor
    picked = total[:up_rows]
    for q in range(1, 128 // up_rows):
        picked = jnp.where(me % (128 // up_rows) == q, total[q * up_rows:(q + 1) * up_rows], picked)
    gu_ref[...] = picked

    for k in range(dp):
        got(out_ref.at[:, k * feats:(k + 1) * feats], o_r.at[k])
    for s in range(dp):
        b = ahead[s]
        to_owner_done(down_out.at[b], down_in.at[slot], d_s.at[b], d_r.at[slot], b)
        to_owner_done(out_buf.at[b], out_ref.at[:, out_cols], o_s.at[b], o_r.at[slot], b)
    for copy in far:
        pl.when(is_inner)(copy.wait_send)
    for copy in sent:
        copy.wait_send()


def finish_kernel(out_in, gd_in, gu_in, out_ref, gd_ref, gu_ref, sems):
    copies = [
        pltpu.make_async_copy(src, dst, sems.at[i])
        for i, (src, dst) in enumerate([(out_in, out_ref), (gd_in, gd_ref), (gu_in, gu_ref)])
    ]
    for copy in copies:
        copy.start()
    for copy in copies:
        copy.wait()


def token_body(
    dp,
    inputs,
    value_output_gradient,
    value_projection_weight,
    adapter_down_factor,
    adapter_up_factor,
    membership,
    active_token_lengths,
):
    tok, heads = value_output_gradient.shape
    jobs, rank, feats = adapter_down_factor.shape
    cols = jobs * rank
    bf16, f32 = jnp.bfloat16, jnp.float32
    vmem = pl.BlockSpec(memory_space=pltpu.VMEM)
    hbm = pl.BlockSpec(memory_space=pltpu.HBM)
    smem = pl.BlockSpec(memory_space=pltpu.SMEM)
    dma = pltpu.SemaphoreType.DMA
    out, gd, gu = pl.pallas_call(
        functools.partial(exchange_kernel, dp, jobs, rank),
        out_shape=(
            jax.ShapeDtypeStruct((tok, dp * feats), bf16),
            jax.ShapeDtypeStruct((cols, feats), f32),
            jax.ShapeDtypeStruct((heads // dp, cols), f32),
        ),
        in_specs=[hbm] * 5 + [smem] * 2,
        out_specs=(pl.BlockSpec(memory_space=pl.ANY), vmem, vmem),
        scratch_shapes=[
            pltpu.VMEM((tok, dp * feats), bf16),
            pltpu.VMEM((tok, heads), bf16),
            pltpu.VMEM((2 * feats, heads), bf16),
            pltpu.VMEM((cols, feats), bf16),
            pltpu.VMEM((cols, heads), bf16),
            pltpu.VMEM((dp, 2, tok, heads), bf16),
            pltpu.VMEM((feats, heads), bf16),
            pltpu.VMEM((cols, heads), bf16),
            pltpu.VMEM((dp, 8, 128), jnp.int32),
            pltpu.VMEM((dp, rank, feats), bf16),
            pltpu.VMEM((dp, rank, feats), bf16),
            pltpu.VMEM((dp, tok, feats), bf16),
            pltpu.VMEM((dp, rank, feats), bf16),
            pltpu.VMEM((dp, rank, feats), bf16),
            pltpu.VMEM((2, rank, tok), f32),
            pltpu.VMEM((dp, rank, tok), bf16),
        ]
        + [dma((5,))]
        + [dma((dp,))] * 8
        + [dma((3,))] * 2
        + [dma((dp,))] * 8,
        compiler_params=pltpu.CompilerParams(
            collective_id=0, has_side_effects=True, vmem_limit_bytes=32 * 2**20
        ),
        cost_estimate=pl.CostEstimate(
            flops=2 * dp * tok * 2 * heads * feats, bytes_accessed=2**23, transcendentals=0
        ),
    )(
        inputs,
        value_output_gradient,
        value_projection_weight,
        adapter_down_factor.reshape(cols, feats),
        adapter_up_factor.reshape(cols, heads),
        membership.reshape(jobs),
        active_token_lengths,
    )
    out, gd, gu = pl.pallas_call(
        finish_kernel,
        out_shape=tuple(jax.ShapeDtypeStruct(a.shape, a.dtype) for a in (out, gd, gu)),
        in_specs=[pl.BlockSpec(memory_space=pl.ANY)] * 3,
        out_specs=(hbm,) * 3,
        scratch_shapes=[dma((3,))],
    )(out, gd, gu)
    return out, gd.T[None], gu[None]


def weight_body(
    inputs,
    value_output_gradient,
    value_projection_weight,
    adapter_down_factor,
    adapter_up_factor,
    membership,
    active_token_lengths,
):
    tok_rows = inputs.shape[0]
    feat_half = inputs.shape[1]
    job_count = membership.shape[0]
    rank_dimension_size = adapter_down_factor.shape[1]
    live_rows = lax.iota(jnp.int32, tok_rows) < active_token_lengths[0]
    grad_masked = jnp.where(
        live_rows[:, None], value_output_gradient, jnp.zeros_like(value_output_gradient)
    )
    own_jobs = membership[:, 0]
    owned_weight_rows = own_jobs.astype(jnp.bfloat16)
    tenant_token_rows = lax.psum(
        own_jobs.astype(jnp.float32) * active_token_lengths[0].astype(jnp.float32), "dp"
    )
    every_down_factor = lax.all_gather(adapter_down_factor, ("dp", "tensor"), axis=2, tiled=True)
    job_down_factor = jnp.einsum(
        "j,jrd->rd", owned_weight_rows, every_down_factor, preferred_element_type=jnp.float32
    ).astype(jnp.bfloat16)
    up_job = jnp.einsum(
        "p,pxh->xh", owned_weight_rows, adapter_up_factor, preferred_element_type=jnp.float32
    ).astype(jnp.bfloat16)
    resident_down_factor = lax.dynamic_slice_in_dim(
        job_down_factor, lax.axis_index("tensor") * feat_half, feat_half, 1
    )
    down_terms = contract_cols(inputs, resident_down_factor)
    up_terms = contract_cols(grad_masked, up_job)
    projected_full, back_full = lax.psum((down_terms, up_terms), "tensor")
    projected = jnp.where(
        live_rows[:, None], projected_full, jnp.zeros_like(projected_full)
    ).astype(jnp.bfloat16)
    rank_gradient_back = back_full.astype(jnp.bfloat16)
    frozen_terms = contract_cols(
        grad_masked, lax.all_gather(value_projection_weight, "dp", axis=0, tiled=True)
    )
    fixed_weight = lax.psum_scatter(
        frozen_terms.astype(jnp.bfloat16), "tensor", scatter_dimension=1, tiled=True
    ).astype(jnp.float32)
    grad_inputs = (
        fixed_weight
        + adapter_scale
        * jnp.dot(rank_gradient_back, resident_down_factor, preferred_element_type=jnp.float32)
    ).astype(jnp.bfloat16)
    wide_cols = job_count * rank_dimension_size
    factor_column_count = jnp.repeat(adapter_scale / tenant_token_rows, rank_dimension_size)
    back_expand = (rank_gradient_back[:, None, :] * owned_weight_rows[None, :, None]).reshape(
        tok_rows, wide_cols
    )
    columns = inputs
    down_sums = lax.psum_scatter(
        contract_rows(columns, back_expand), "dp", scatter_dimension=0, tiled=True
    )
    proj_expand = (projected[:, None, :] * owned_weight_rows[None, :, None]).reshape(
        tok_rows, wide_cols
    )
    columns = grad_masked
    up_sums = lax.psum_scatter(
        contract_rows(columns, proj_expand), "dp", scatter_dimension=0, tiled=True
    )
    grad_down = (down_sums * factor_column_count[None, :])[None]
    grad_up = (up_sums * factor_column_count[None, :])[None]
    return (grad_inputs, grad_down, grad_up)


def solution(mesh):
    in_specs = (
        P(("groups", "dp"), "tensor"),
        P(("groups", "dp"), "tensor"),
        P("dp", "tensor"),
        P(None, None, ("dp", "tensor")),
        P(None, None, "tensor"),
        P(None, ("groups", "dp")),
        P(("groups", "dp")),
    )
    out_specs = (
        P(("groups", "dp"), "tensor"),
        P("tensor", ("groups", "dp"), None),
        P("tensor", ("groups", "dp"), None),
    )

    def body(*args):
        dp = mesh.shape["dp"]
        tok, heads = args[1].shape
        jobs, rank, feats = args[3].shape
        tokens_travel = (
            args[2].shape[0] > tok
            and mesh.shape["tensor"] == 2
            and dp == 8
            and args[2].shape[0] == 2 * feats
            and tok == 128
            and rank == 16
            and jobs * rank <= 128
            and jobs <= 6
            and feats % 128 == 0
            and heads % (8 * dp) == 0
            and 128 % (heads // dp) == 0
        )
        if tokens_travel:
            return token_body(dp, *args)
        return weight_body(*args)

    return jax.shard_map(body, mesh=mesh, in_specs=in_specs, out_specs=out_specs, check_vma=False)
```

```python
import functools

import jax
import jax.numpy as jnp
from jax import lax
from jax.experimental import pallas as pl
from jax.experimental.pallas import tpu as pltpu
from jax.sharding import PartitionSpec as P

adapter_scale = 2.0
MESH = pl.DeviceIdType.MESH


def contract_rows(left, right):
    return lax.dot_general(
        left, right, (((0,), (0,)), ((), ())), preferred_element_type=jnp.float32
    )


def contract_cols(left, right):
    return lax.dot_general(
        left, right, (((1,), (1,)), ((), ())), preferred_element_type=jnp.float32
    )


def plain_dot(left, right):
    return jnp.dot(left, right, preferred_element_type=jnp.float32)


def wide(row, lanes):
    return jnp.concatenate([row] * (lanes // row.shape[1]), axis=1)


def exchange_kernel(
    dp,
    jobs,
    rank,
    x_hbm,
    g_hbm,
    w_hbm,
    down_hbm,
    up_hbm,
    member_ref,
    length_ref,
    out_ref,
    gd_ref,
    gu_ref,
    x_ref, g_ref, w_ref, down_ref, up_ref,
    grads,
    w_sib,
    up_sib,
    meta,
    down_out,
    down_in,
    out_buf,
    part_out,
    part_in,
    proj_half,
    proj,
    load_s, meta_s, meta_r, g_s, g_r, f_s, zf_s, gf_s, gf_r, one_s, one_r,
    d_s, d_r, o_s, o_r, p_s, p_r, j_s, j_r,
):
    tok, heads = g_ref.shape
    feats = down_ref.shape[1]
    cols = jobs * rank
    gi, me, core = lax.axis_index("groups"), lax.axis_index("dp"), lax.axis_index("tensor")
    other = 1 - core
    depth = dp // 2
    z, x = me // 2, me % 2
    owner_core = me // depth
    slot = (2 * me + core) % dp
    ahead = [lax.rem(me + s, dp) for s in range(dp)]

    def remote(src, dst, send, recv, to_dp, to_core):
        return pltpu.make_async_remote_copy(
            src_ref=src, dst_ref=dst, send_sem=send, recv_sem=recv,
            device_id=(gi, to_dp, to_core), device_id_type=MESH,
        )

    loads = [
        pltpu.make_async_copy(src, dst, load_s.at[i])
        for i, (src, dst) in enumerate(
            [(g_hbm, g_ref), (up_hbm, up_ref), (down_hbm, down_ref), (w_hbm, w_ref), (x_hbm, x_ref)]
        )
    ]
    for load in loads:
        load.start()

    barrier = pltpu.get_barrier_semaphore()
    for s in range(dp):
        for c in range(2):
            if s == 0 and c == 1:
                continue
            to_core = other if s == 0 else c
            pl.semaphore_signal(
                barrier, inc=1, device_id=(gi, ahead[s], to_core), device_id_type=MESH
            )

    row = lax.broadcasted_iota(jnp.int32, (8, 128), 0)
    column = lax.broadcasted_iota(jnp.int32, (8, 128), 1)
    marks = (row == jobs).astype(jnp.int32) * length_ref[0]
    for j in range(jobs):
        by_column = jnp.logical_and(row == jobs + 1, column // rank == j)
        marks = marks + jnp.logical_or(row == j, by_column).astype(jnp.int32) * member_ref[j]
    meta[me] = marks
    length = meta[me, jobs:jobs + 1, :]
    live = lax.broadcasted_iota(jnp.int32, (tok, heads), 0) < wide(length, heads)
    loads[0].wait()
    grads[me, core] = jnp.where(live, g_ref[...], jnp.zeros_like(g_ref))
    loads[1].wait()
    pl.semaphore_wait(barrier, 2 * dp - 1)

    sent = []

    def go(copy):
        copy.start()
        sent.append(copy)

    pair, inner_far, end_far = z ^ 1, jnp.where(z < depth // 2, 2, 1), jnp.where(z < depth // 2, 3, 0)
    is_inner = jnp.logical_or(z == 1, z == 2)
    beside, paired = z * 2 + (1 - x), pair * 2 + x
    own = grads.at[me, core]
    go(remote(own, own, gf_s.at[me], gf_r.at[me], me, other))
    go(remote(up_ref, up_sib, one_s.at[0], one_r.at[0], me, other))
    for s in range(1, dp):
        go(remote(meta.at[me], meta.at[me], meta_s.at[ahead[s]], meta_r.at[me], ahead[s], core))
    for to in (inner_far * 2 + x, paired, beside):
        go(remote(own, own, g_s.at[to], g_r.at[me], to, core))
    loads[3].wait()
    w_half = w_ref.at[pl.ds(pl.multiple_of(other * feats, feats), feats), :]
    go(remote(w_half, w_sib, one_s.at[1], one_r.at[1], me, other))

    def got(dst, recv):
        remote(dst, dst, one_s.at[0], recv, me, other).wait_recv()

    def pick(rows, b):
        n = rows.shape[1]
        total = jnp.zeros((rank, n), jnp.float32)
        for j in range(jobs):
            held = meta[b, j:j + 1, :].astype(jnp.float32)
            total = total + rows[j * rank:(j + 1) * rank, :].astype(jnp.float32) * wide(held, n)
        return total.astype(jnp.bfloat16)

    got(up_sib, one_r.at[0])
    got(grads.at[me, other], gf_r.at[me])
    up_own, up_other = up_ref[...], up_sib[...]
    back = contract_cols(pick(up_own, me), grads[me, core]) + contract_cols(
        pick(up_other, me), grads[me, other]
    )
    back = back.astype(jnp.bfloat16)
    loads[4].wait()
    for b in range(dp):
        part_out[b] = plain_dot(back, x_ref[:, b * feats:(b + 1) * feats]).astype(jnp.bfloat16)
    part_in[me] = part_out[me]
    for s in range(1, dp):
        got(meta.at[ahead[s]], meta_r.at[ahead[s]])
    loads[2].wait()
    down_all = down_ref[...]
    for b in range(dp):
        down_out[b] = pick(down_all, b)

    mine = owner_core == core

    def to_owner(src, dst, send, recv, b):
        @pl.when(jnp.logical_and(b == me, mine))
        def _():
            pltpu.make_async_copy(src, dst, recv).start()

        @pl.when(jnp.logical_not(jnp.logical_and(b == me, mine)))
        def _():
            remote(src, dst, send, recv, b, owner_core).start()

    def to_owner_done(src, dst, send, recv, b):
        @pl.when(jnp.logical_not(jnp.logical_and(b == me, mine)))
        def _():
            remote(src, dst, send, recv, b, owner_core).wait_send()

    for s in range(dp):
        b = ahead[s]
        to_owner(down_out.at[b], down_in.at[slot], d_s.at[b], d_r.at[slot], b)
    for s in range(1, dp):
        b = ahead[s]
        go(remote(part_out.at[b], part_in.at[me], p_s.at[b], p_r.at[me], b, core))

    got(w_sib, one_r.at[1])
    w_own = w_ref.at[pl.ds(pl.multiple_of(core * feats, feats), feats), :]
    out_cols = pl.ds(pl.multiple_of(slot * feats, feats), feats)

    far = []

    def arrive(zs, dx, direct=False):
        b = zs * 2 + (x if dx == 0 else 1 - x)
        block = grads.at[b, core]
        got(block, g_r.at[b])
        if direct:
            copy = remote(block, block, zf_s.at[b], g_r.at[b], paired, core)
            pl.when(is_inner)(copy.start)
            far.append(copy)
        go(remote(block, block, gf_s.at[b], gf_r.at[b], me, other))
        if dx == 0:
            go(remote(block, block, f_s.at[b], g_r.at[b], beside, core))
        return b

    def block_out(b, wait_half):
        if wait_half:
            got(grads.at[b, other], gf_r.at[b])
        g_own, g_other = grads[b, core], grads[b, other]
        frozen = contract_cols(g_own, w_own[...]) + contract_cols(g_other, w_sib[...])
        rb = contract_cols(g_own, up_own) + contract_cols(g_other, up_other)
        held = meta[b, jobs + 1:jobs + 2, :cols].astype(jnp.float32)
        rb = (rb.astype(jnp.bfloat16).astype(jnp.float32) * held).astype(jnp.bfloat16)
        out_buf[b] = (frozen + adapter_scale * plain_dot(rb, down_all)).astype(jnp.bfloat16)
        to_owner(out_buf.at[b], out_ref.at[:, out_cols], o_s.at[b], o_r.at[slot], b)

    order = [
        (inner_far, 0, True), (pair, 0), (end_far, 0, True), (z, 1),
        (inner_far, 1), (pair, 1), (end_far, 1), None,
    ]
    held_b = arrive(*order[0])
    for i in range(dp):
        later = me
        if i + 1 < dp and order[i + 1] is not None:
            later = arrive(*order[i + 1])
        block_out(held_b, order[i] is not None)
        held_b = later
        if i == depth - 1:
            total = jnp.zeros((rank, tok), jnp.float32)
            for k in range(dp):
                got(down_in.at[k], d_r.at[k])
                total = total + contract_cols(down_in[k], x_ref[:, k * feats:(k + 1) * feats])
            proj_half[core] = total
            half = proj_half.at[core]
            go(remote(half, half, one_s.at[2], one_r.at[2], me, other))
        if i == depth:
            got(proj_half.at[other], one_r.at[2])
            full = proj_half[0] + proj_half[1]
            alive = lax.broadcasted_iota(jnp.int32, (rank, tok), 1) < length
            proj[me] = jnp.where(alive, full, jnp.zeros_like(full)).astype(jnp.bfloat16)
            for s in range(1, dp):
                go(remote(proj.at[me], proj.at[me], j_s.at[ahead[s]], j_r.at[me], ahead[s], core))

    tokens = jnp.zeros((1, 128), jnp.float32)
    for b in range(dp):
        tokens = tokens + (meta[b, jobs + 1:jobs + 2, :] * meta[b, jobs:jobs + 1, :]).astype(jnp.float32)
    factor = adapter_scale / tokens[:, :cols]

    for s in range(1, dp):
        got(part_in.at[ahead[s]], p_r.at[ahead[s]])
    same = (
        lax.broadcasted_iota(jnp.int32, (rank, 128), 1) % rank
        == lax.broadcasted_iota(jnp.int32, (rank, 128), 0)
    ).astype(jnp.float32)
    place = jnp.concatenate(
        [same * meta[b, jobs + 1:jobs + 2, :].astype(jnp.float32) for b in range(dp)], axis=0
    ).astype(jnp.bfloat16)
    parts = part_in[...].reshape(dp * rank, feats)
    sums = contract_rows(place, parts)
    for j in range(jobs):
        held = jnp.zeros((1, 128), jnp.float32)
        for b in range(dp):
            held = held + (meta[b, j:j + 1, :] * meta[b, jobs:jobs + 1, :]).astype(jnp.float32)
        gd_ref[j * rank:(j + 1) * rank, :] = sums[j * rank:(j + 1) * rank, :] * wide(
            adapter_scale / held, feats
        )

    up_rows = heads // dp
    first = pl.multiple_of((me * up_rows) // 128 * 128, 128)
    total = jnp.zeros((128, cols), jnp.float32)
    for s in range(dp):
        b = ahead[s]
        if s:
            got(proj.at[b], j_r.at[b])
        p_b = proj[b].astype(jnp.float32)
        spread = jnp.concatenate(
            [p_b * meta[b, j:j + 1, :].astype(jnp.float32) for j in range(jobs)], axis=0
        ).astype(jnp.bfloat16)
        g_b = grads[b, core, :, pl.ds(first, 128)]
        total = total + lax.dot_general(
            g_b, spread, (((0,), (1,)), ((), ())), preferred_element_type=jnp.float32
        )
    total = total * factor
    picked = total[:up_rows]
    for q in range(1, 128 // up_rows):
        picked = jnp.where(me % (128 // up_rows) == q, total[q * up_rows:(q + 1) * up_rows], picked)
    gu_ref[...] = picked

    for k in range(dp):
        got(out_ref.at[:, k * feats:(k + 1) * feats], o_r.at[k])
    for s in range(dp):
        b = ahead[s]
        to_owner_done(down_out.at[b], down_in.at[slot], d_s.at[b], d_r.at[slot], b)
        to_owner_done(out_buf.at[b], out_ref.at[:, out_cols], o_s.at[b], o_r.at[slot], b)
    for copy in far:
        pl.when(is_inner)(copy.wait_send)
    for copy in sent:
        copy.wait_send()


def finish_kernel(out_in, gd_in, gu_in, out_ref, gd_ref, gu_ref):
    out_ref[...] = out_in[...]
    gd_ref[...] = gd_in[...]
    gu_ref[...] = gu_in[...]


def token_body(
    dp,
    inputs,
    value_output_gradient,
    value_projection_weight,
    adapter_down_factor,
    adapter_up_factor,
    membership,
    active_token_lengths,
):
    tok, heads = value_output_gradient.shape
    jobs, rank, feats = adapter_down_factor.shape
    cols = jobs * rank
    bf16, f32 = jnp.bfloat16, jnp.float32
    vmem = pl.BlockSpec(memory_space=pltpu.VMEM)
    hbm = pl.BlockSpec(memory_space=pltpu.HBM)
    smem = pl.BlockSpec(memory_space=pltpu.SMEM)
    dma = pltpu.SemaphoreType.DMA
    out, gd, gu = pl.pallas_call(
        functools.partial(exchange_kernel, dp, jobs, rank),
        out_shape=(
            jax.ShapeDtypeStruct((tok, dp * feats), bf16),
            jax.ShapeDtypeStruct((cols, feats), f32),
            jax.ShapeDtypeStruct((heads // dp, cols), f32),
        ),
        in_specs=[hbm] * 5 + [smem] * 2,
        out_specs=(pl.BlockSpec(memory_space=pl.ANY), vmem, vmem),
        scratch_shapes=[
            pltpu.VMEM((tok, dp * feats), bf16),
            pltpu.VMEM((tok, heads), bf16),
            pltpu.VMEM((2 * feats, heads), bf16),
            pltpu.VMEM((cols, feats), bf16),
            pltpu.VMEM((cols, heads), bf16),
            pltpu.VMEM((dp, 2, tok, heads), bf16),
            pltpu.VMEM((feats, heads), bf16),
            pltpu.VMEM((cols, heads), bf16),
            pltpu.VMEM((dp, 8, 128), jnp.int32),
            pltpu.VMEM((dp, rank, feats), bf16),
            pltpu.VMEM((dp, rank, feats), bf16),
            pltpu.VMEM((dp, tok, feats), bf16),
            pltpu.VMEM((dp, rank, feats), bf16),
            pltpu.VMEM((dp, rank, feats), bf16),
            pltpu.VMEM((2, rank, tok), f32),
            pltpu.VMEM((dp, rank, tok), bf16),
        ]
        + [dma((5,))]
        + [dma((dp,))] * 8
        + [dma((3,))] * 2
        + [dma((dp,))] * 8,
        compiler_params=pltpu.CompilerParams(
            collective_id=0, has_side_effects=True, vmem_limit_bytes=60 * 2**20
        ),
        cost_estimate=pl.CostEstimate(
            flops=2 * dp * tok * 2 * heads * feats, bytes_accessed=2**23, transcendentals=0
        ),
    )(
        inputs,
        value_output_gradient,
        value_projection_weight,
        adapter_down_factor.reshape(cols, feats),
        adapter_up_factor.reshape(cols, heads),
        membership.reshape(jobs),
        active_token_lengths,
    )
    grid = 2
    blocks = (
        pl.BlockSpec((tok, dp * feats // grid), lambda i: (0, i)),
        pl.BlockSpec((cols, feats // grid), lambda i: (0, i)),
        pl.BlockSpec((heads // dp, cols), lambda i: (0, 0)),
    )
    out, gd, gu = pl.pallas_call(
        finish_kernel,
        grid=(grid,),
        out_shape=tuple(jax.ShapeDtypeStruct(a.shape, a.dtype) for a in (out, gd, gu)),
        in_specs=blocks,
        out_specs=blocks,
        compiler_params=pltpu.CompilerParams(vmem_limit_bytes=60 * 2**20),
    )(out, gd, gu)
    return out, gd.T[None], gu[None]


def weight_body(
    inputs,
    value_output_gradient,
    value_projection_weight,
    adapter_down_factor,
    adapter_up_factor,
    membership,
    active_token_lengths,
):
    tok_rows = inputs.shape[0]
    feat_half = inputs.shape[1]
    job_count = membership.shape[0]
    rank_dimension_size = adapter_down_factor.shape[1]
    live_rows = lax.iota(jnp.int32, tok_rows) < active_token_lengths[0]
    grad_masked = jnp.where(
        live_rows[:, None], value_output_gradient, jnp.zeros_like(value_output_gradient)
    )
    own_jobs = membership[:, 0]
    owned_weight_rows = own_jobs.astype(jnp.bfloat16)
    tenant_token_rows = lax.psum(
        own_jobs.astype(jnp.float32) * active_token_lengths[0].astype(jnp.float32), "dp"
    )
    every_down_factor = lax.all_gather(adapter_down_factor, ("dp", "tensor"), axis=2, tiled=True)
    job_down_factor = jnp.einsum(
        "j,jrd->rd", owned_weight_rows, every_down_factor, preferred_element_type=jnp.float32
    ).astype(jnp.bfloat16)
    up_job = jnp.einsum(
        "p,pxh->xh", owned_weight_rows, adapter_up_factor, preferred_element_type=jnp.float32
    ).astype(jnp.bfloat16)
    resident_down_factor = lax.dynamic_slice_in_dim(
        job_down_factor, lax.axis_index("tensor") * feat_half, feat_half, 1
    )
    down_terms = contract_cols(inputs, resident_down_factor)
    up_terms = contract_cols(grad_masked, up_job)
    projected_full, back_full = lax.psum((down_terms, up_terms), "tensor")
    projected = jnp.where(
        live_rows[:, None], projected_full, jnp.zeros_like(projected_full)
    ).astype(jnp.bfloat16)
    rank_gradient_back = back_full.astype(jnp.bfloat16)
    frozen_terms = contract_cols(
        grad_masked, lax.all_gather(value_projection_weight, "dp", axis=0, tiled=True)
    )
    fixed_weight = lax.psum_scatter(
        frozen_terms.astype(jnp.bfloat16), "tensor", scatter_dimension=1, tiled=True
    ).astype(jnp.float32)
    grad_inputs = (
        fixed_weight
        + adapter_scale
        * jnp.dot(rank_gradient_back, resident_down_factor, preferred_element_type=jnp.float32)
    ).astype(jnp.bfloat16)
    wide_cols = job_count * rank_dimension_size
    factor_column_count = jnp.repeat(adapter_scale / tenant_token_rows, rank_dimension_size)
    back_expand = (rank_gradient_back[:, None, :] * owned_weight_rows[None, :, None]).reshape(
        tok_rows, wide_cols
    )
    columns = inputs
    down_sums = lax.psum_scatter(
        contract_rows(columns, back_expand), "dp", scatter_dimension=0, tiled=True
    )
    proj_expand = (projected[:, None, :] * owned_weight_rows[None, :, None]).reshape(
        tok_rows, wide_cols
    )
    columns = grad_masked
    up_sums = lax.psum_scatter(
        contract_rows(columns, proj_expand), "dp", scatter_dimension=0, tiled=True
    )
    grad_down = (down_sums * factor_column_count[None, :])[None]
    grad_up = (up_sums * factor_column_count[None, :])[None]
    return (grad_inputs, grad_down, grad_up)


def solution(mesh):
    in_specs = (
        P(("groups", "dp"), "tensor"),
        P(("groups", "dp"), "tensor"),
        P("dp", "tensor"),
        P(None, None, ("dp", "tensor")),
        P(None, None, "tensor"),
        P(None, ("groups", "dp")),
        P(("groups", "dp")),
    )
    out_specs = (
        P(("groups", "dp"), "tensor"),
        P("tensor", ("groups", "dp"), None),
        P("tensor", ("groups", "dp"), None),
    )

    def body(*args):
        dp = mesh.shape["dp"]
        tok, heads = args[1].shape
        jobs, rank, feats = args[3].shape
        tokens_travel = (
            args[2].shape[0] > tok
            and mesh.shape["tensor"] == 2
            and dp == 8
            and args[2].shape[0] == 2 * feats
            and tok == 128
            and rank == 16
            and jobs * rank <= 128
            and jobs <= 6
            and feats % 128 == 0
            and heads % (8 * dp) == 0
            and 128 % (heads // dp) == 0
        )
        if tokens_travel:
            return token_body(dp, *args)
        return weight_body(*args)

    return jax.shard_map(body, mesh=mesh, in_specs=in_specs, out_specs=out_specs, check_vma=False)
```

```python
import functools

import jax
import jax.numpy as jnp
from jax import lax
from jax.experimental import pallas as pl
from jax.experimental.pallas import tpu as pltpu
from jax.sharding import PartitionSpec as P

adapter_scale = 2.0
cuts = 2
MESH = pl.DeviceIdType.MESH


def contract_rows(left, right):
    return lax.dot_general(
        left, right, (((0,), (0,)), ((), ())), preferred_element_type=jnp.float32
    )


def contract_cols(left, right):
    return lax.dot_general(
        left, right, (((1,), (1,)), ((), ())), preferred_element_type=jnp.float32
    )


def plain_dot(left, right):
    return jnp.dot(left, right, preferred_element_type=jnp.float32)


def wide(row, lanes):
    return jnp.concatenate([row] * (lanes // row.shape[1]), axis=1)


def exchange_kernel(
    dp,
    jobs,
    rank,
    x_hbm,
    g_hbm,
    w_hbm,
    down_hbm,
    up_hbm,
    member_ref,
    length_ref,
    out_ref,
    gd_ref,
    gu_ref,
    x_ref, g_ref, w_ref, down_ref, up_ref,
    grads,
    w_sib,
    up_sib,
    meta,
    down_out,
    down_in,
    out_buf,
    part_out,
    part_in,
    proj_half,
    proj,
    load_s, meta_s, meta_r, g_s, g_r, f_s, zf_s, gf_s, gf_r, one_s, one_r,
    d_s, d_r, o_s, o_r, p_s, p_r, j_s, j_r,
):
    tok, heads = g_ref.shape
    feats = down_ref.shape[1]
    cols = jobs * rank
    gi, me, core = lax.axis_index("groups"), lax.axis_index("dp"), lax.axis_index("tensor")
    other = 1 - core
    depth = dp // 2
    z, x = me // 2, me % 2
    owner_core = me // depth
    slot = (2 * me + core) % dp
    ahead = [lax.rem(me + s, dp) for s in range(dp)]

    def remote(src, dst, send, recv, to_dp, to_core):
        return pltpu.make_async_remote_copy(
            src_ref=src, dst_ref=dst, send_sem=send, recv_sem=recv,
            device_id=(gi, to_dp, to_core), device_id_type=MESH,
        )

    loads = [
        pltpu.make_async_copy(src, dst, load_s.at[i])
        for i, (src, dst) in enumerate(
            [(g_hbm, g_ref), (up_hbm, up_ref), (down_hbm, down_ref), (w_hbm, w_ref), (x_hbm, x_ref)]
        )
    ]
    for load in loads:
        load.start()

    barrier = pltpu.get_barrier_semaphore()
    for s in range(dp):
        for c in range(2):
            if s == 0 and c == 1:
                continue
            to_core = other if s == 0 else c
            pl.semaphore_signal(
                barrier, inc=1, device_id=(gi, ahead[s], to_core), device_id_type=MESH
            )

    column = lax.broadcasted_iota(jnp.int32, (1, 128), 1)
    marks = (column >= cols).astype(jnp.int32) * length_ref[0]
    for j in range(jobs):
        marks = marks + (column // rank == j).astype(jnp.int32) * member_ref[j]
    meta[me] = marks
    length = jnp.zeros((1, 128), jnp.int32) + length_ref[0]
    live = lax.broadcasted_iota(jnp.int32, (tok, heads), 0) < wide(length, heads)
    loads[0].wait()
    grads[me, core] = jnp.where(live, g_ref[...], jnp.zeros_like(g_ref))
    loads[1].wait()
    pl.semaphore_wait(barrier, 2 * dp - 1)

    sent = []

    def go(copy):
        copy.start()
        sent.append(copy)

    pair, inner_far, end_far = z ^ 1, jnp.where(z < depth // 2, 2, 1), jnp.where(z < depth // 2, 3, 0)
    is_inner = jnp.logical_or(z == 1, z == 2)
    beside, paired = z * 2 + (1 - x), pair * 2 + x
    height = tok // cuts

    def cut(b, c, h):
        return grads.at[b, c, h * height:(h + 1) * height, :]

    for h in range(cuts):
        own, n = cut(me, core, h), me * cuts + h
        go(remote(own, own, gf_s.at[n], gf_r.at[n], me, other))
    go(remote(up_ref, up_sib, one_s.at[0], one_r.at[0], me, other))
    for s in range(1, dp):
        go(remote(meta.at[me], meta.at[me], meta_s.at[ahead[s]], meta_r.at[me], ahead[s], core))
    for to in (inner_far * 2 + x, paired, beside):
        for h in range(cuts):
            own = cut(me, core, h)
            go(remote(own, own, g_s.at[to * cuts + h], g_r.at[me * cuts + h], to, core))
    loads[3].wait()
    w_half = w_ref.at[pl.ds(pl.multiple_of(other * feats, feats), feats), :]
    go(remote(w_half, w_sib, one_s.at[1], one_r.at[1], me, other))

    def got(dst, recv):
        remote(dst, dst, one_s.at[0], recv, me, other).wait_recv()

    def pick(rows, held_of):
        n = rows.shape[1]
        total = jnp.zeros((rank, n), jnp.float32)
        for j in range(jobs):
            held = held_of(j)
            total = total + rows[j * rank:(j + 1) * rank, :].astype(jnp.float32) * wide(held, n)
        return total.astype(jnp.bfloat16)

    def own_held(j):
        return jnp.zeros((1, 128), jnp.float32) + member_ref[j].astype(jnp.float32)

    got(up_sib, one_r.at[0])
    for h in range(cuts):
        got(cut(me, other, h), gf_r.at[me * cuts + h])
    up_own, up_other = up_ref[...], up_sib[...]
    back = contract_cols(pick(up_own, own_held), grads[me, core]) + contract_cols(
        pick(up_other, own_held), grads[me, other]
    )
    back = back.astype(jnp.bfloat16)
    loads[4].wait()
    for b in range(dp):
        part_out[b] = plain_dot(back, x_ref[:, b * feats:(b + 1) * feats]).astype(jnp.bfloat16)
    part_in[me] = part_out[me]
    for s in range(1, dp):
        got(meta.at[ahead[s]], meta_r.at[ahead[s]])
    all_marks = meta[...].reshape(dp, 128).astype(jnp.float32)
    lanes = lax.broadcasted_iota(jnp.int32, (dp, 128), 1)

    def spread(lane):
        one = jnp.where(lanes == lane, all_marks, jnp.zeros_like(all_marks))
        return jnp.broadcast_to(jnp.sum(one, axis=1, keepdims=True), (dp, 128))

    holds = [spread(j * rank) for j in range(jobs)]
    lengths = spread(cols)
    loads[2].wait()
    down_all = down_ref[...]
    for b in range(dp):
        down_out[b] = pick(down_all, lambda j: holds[j][b:b + 1, :])

    mine = owner_core == core

    def to_owner(src, dst, send, recv, b):
        @pl.when(jnp.logical_and(b == me, mine))
        def _():
            pltpu.make_async_copy(src, dst, recv).start()

        @pl.when(jnp.logical_not(jnp.logical_and(b == me, mine)))
        def _():
            remote(src, dst, send, recv, b, owner_core).start()

    def to_owner_done(src, dst, send, recv, b):
        @pl.when(jnp.logical_not(jnp.logical_and(b == me, mine)))
        def _():
            remote(src, dst, send, recv, b, owner_core).wait_send()

    for s in range(dp):
        b = ahead[s]
        to_owner(down_out.at[b], down_in.at[slot], d_s.at[b], d_r.at[slot], b)
    for s in range(1, dp):
        b = ahead[s]
        go(remote(part_out.at[b], part_in.at[me], p_s.at[b], p_r.at[me], b, core))

    got(w_sib, one_r.at[1])
    w_own = w_ref.at[pl.ds(pl.multiple_of(core * feats, feats), feats), :]
    out_cols = pl.ds(pl.multiple_of(slot * feats, feats), feats)

    far = []

    def arrive(zs, dx, direct=False):
        b = zs * 2 + (x if dx == 0 else 1 - x)
        for h in range(cuts):
            block, n = cut(b, core, h), b * cuts + h
            got(block, g_r.at[n])
            if direct:
                copy = remote(block, block, zf_s.at[n], g_r.at[n], paired, core)
                pl.when(is_inner)(copy.start)
                far.append(copy)
            if dx == 0:
                go(remote(block, block, f_s.at[n], g_r.at[n], beside, core))
            go(remote(block, block, gf_s.at[n], gf_r.at[n], me, other))
        return b

    def block_out(b, wait_half):
        if wait_half:
            for h in range(cuts):
                got(cut(b, other, h), gf_r.at[b * cuts + h])
        g_own, g_other = grads[b, core], grads[b, other]
        frozen = contract_cols(g_own, w_own[...]) + contract_cols(g_other, w_sib[...])
        rb = contract_cols(g_own, up_own) + contract_cols(g_other, up_other)
        held = meta[b][:, :cols].astype(jnp.float32)
        rb = (rb.astype(jnp.bfloat16).astype(jnp.float32) * held).astype(jnp.bfloat16)
        out_buf[b] = (frozen + adapter_scale * plain_dot(rb, down_all)).astype(jnp.bfloat16)
        to_owner(out_buf.at[b], out_ref.at[:, out_cols], o_s.at[b], o_r.at[slot], b)

    order = [
        (inner_far, 0, True), (pair, 0), (end_far, 0, True), (z, 1),
        (inner_far, 1), (pair, 1), (end_far, 1), None,
    ]
    held_b = arrive(*order[0])
    for i in range(dp):
        later = me
        if i + 1 < dp and order[i + 1] is not None:
            later = arrive(*order[i + 1])
        block_out(held_b, order[i] is not None)
        held_b = later
        if i == depth - 1:
            total = jnp.zeros((rank, tok), jnp.float32)
            for k in range(dp):
                got(down_in.at[k], d_r.at[k])
                total = total + contract_cols(down_in[k], x_ref[:, k * feats:(k + 1) * feats])
            proj_half[core] = total
            half = proj_half.at[core]
            go(remote(half, half, one_s.at[2], one_r.at[2], me, other))
        if i == depth:
            got(proj_half.at[other], one_r.at[2])
            full = proj_half[0] + proj_half[1]
            alive = lax.broadcasted_iota(jnp.int32, (rank, tok), 1) < length
            proj[me] = jnp.where(alive, full, jnp.zeros_like(full)).astype(jnp.bfloat16)
            for s in range(1, dp):
                go(remote(proj.at[me], proj.at[me], j_s.at[ahead[s]], j_r.at[me], ahead[s], core))

    tokens = jnp.sum(all_marks * lengths, axis=0, keepdims=True)
    factor = adapter_scale / tokens[:, :cols]

    for s in range(1, dp):
        got(part_in.at[ahead[s]], p_r.at[ahead[s]])
    same = (
        lax.broadcasted_iota(jnp.int32, (rank, 128), 1) % rank
        == lax.broadcasted_iota(jnp.int32, (rank, 128), 0)
    ).astype(jnp.float32)
    place = jnp.concatenate(
        [same * all_marks[b:b + 1, :] for b in range(dp)], axis=0
    ).astype(jnp.bfloat16)
    parts = part_in[...].reshape(dp * rank, feats)
    sums = contract_rows(place, parts)
    for j in range(jobs):
        held = jnp.sum(holds[j] * lengths, axis=0, keepdims=True)
        gd_ref[j * rank:(j + 1) * rank, :] = sums[j * rank:(j + 1) * rank, :] * wide(
            adapter_scale / held, feats
        )

    up_rows = heads // dp
    first = pl.multiple_of((me * up_rows) // 128 * 128, 128)
    total = jnp.zeros((128, cols), jnp.float32)
    for s in range(1, dp):
        got(proj.at[ahead[s]], j_r.at[ahead[s]])
    for b in range(dp):
        p_b = proj[b].astype(jnp.float32)
        wide_p = jnp.concatenate(
            [p_b * holds[j][b:b + 1, :] for j in range(jobs)], axis=0
        ).astype(jnp.bfloat16)
        g_b = grads[b, core, :, pl.ds(first, 128)]
        total = total + lax.dot_general(
            g_b, wide_p, (((0,), (1,)), ((), ())), preferred_element_type=jnp.float32
        )
    total = total * factor
    picked = total[:up_rows]
    for q in range(1, 128 // up_rows):
        picked = jnp.where(me % (128 // up_rows) == q, total[q * up_rows:(q + 1) * up_rows], picked)
    gu_ref[...] = picked

    for k in range(dp):
        got(out_ref.at[:, k * feats:(k + 1) * feats], o_r.at[k])
    for s in range(dp):
        b = ahead[s]
        to_owner_done(down_out.at[b], down_in.at[slot], d_s.at[b], d_r.at[slot], b)
        to_owner_done(out_buf.at[b], out_ref.at[:, out_cols], o_s.at[b], o_r.at[slot], b)
    for copy in far:
        pl.when(is_inner)(copy.wait_send)
    for copy in sent:
        copy.wait_send()


def finish_kernel(out_in, gd_in, gu_in, out_ref, gd_ref, gu_ref):
    out_ref[...] = out_in[...]
    gd_ref[...] = gd_in[...]
    gu_ref[...] = gu_in[...]


def token_body(
    dp,
    inputs,
    value_output_gradient,
    value_projection_weight,
    adapter_down_factor,
    adapter_up_factor,
    membership,
    active_token_lengths,
):
    tok, heads = value_output_gradient.shape
    jobs, rank, feats = adapter_down_factor.shape
    cols = jobs * rank
    bf16, f32 = jnp.bfloat16, jnp.float32
    vmem = pl.BlockSpec(memory_space=pltpu.VMEM)
    hbm = pl.BlockSpec(memory_space=pltpu.HBM)
    smem = pl.BlockSpec(memory_space=pltpu.SMEM)
    dma = pltpu.SemaphoreType.DMA
    out, gd, gu = pl.pallas_call(
        functools.partial(exchange_kernel, dp, jobs, rank),
        out_shape=(
            jax.ShapeDtypeStruct((tok, dp * feats), bf16),
            jax.ShapeDtypeStruct((cols, feats), f32),
            jax.ShapeDtypeStruct((heads // dp, cols), f32),
        ),
        in_specs=[hbm] * 5 + [smem] * 2,
        out_specs=(pl.BlockSpec(memory_space=pl.ANY), vmem, vmem),
        scratch_shapes=[
            pltpu.VMEM((tok, dp * feats), bf16),
            pltpu.VMEM((tok, heads), bf16),
            pltpu.VMEM((2 * feats, heads), bf16),
            pltpu.VMEM((cols, feats), bf16),
            pltpu.VMEM((cols, heads), bf16),
            pltpu.VMEM((dp, 2, tok, heads), bf16),
            pltpu.VMEM((feats, heads), bf16),
            pltpu.VMEM((cols, heads), bf16),
            pltpu.VMEM((dp, 1, 128), jnp.int32),
            pltpu.VMEM((dp, rank, feats), bf16),
            pltpu.VMEM((dp, rank, feats), bf16),
            pltpu.VMEM((dp, tok, feats), bf16),
            pltpu.VMEM((dp, rank, feats), bf16),
            pltpu.VMEM((dp, rank, feats), bf16),
            pltpu.VMEM((2, rank, tok), f32),
            pltpu.VMEM((dp, rank, tok), bf16),
        ]
        + [dma((5,))]
        + [dma((dp,))] * 2
        + [dma((dp * cuts,))] * 6
        + [dma((3,))] * 2
        + [dma((dp,))] * 8,
        compiler_params=pltpu.CompilerParams(
            collective_id=0, has_side_effects=True, vmem_limit_bytes=60 * 2**20
        ),
        cost_estimate=pl.CostEstimate(
            flops=2 * dp * tok * 2 * heads * feats, bytes_accessed=2**23, transcendentals=0
        ),
    )(
        inputs,
        value_output_gradient,
        value_projection_weight,
        adapter_down_factor.reshape(cols, feats),
        adapter_up_factor.reshape(cols, heads),
        membership.reshape(jobs),
        active_token_lengths,
    )
    grid = 2
    blocks = (
        pl.BlockSpec((tok, dp * feats // grid), lambda i: (0, i)),
        pl.BlockSpec((cols, feats // grid), lambda i: (0, i)),
        pl.BlockSpec((heads // dp, cols), lambda i: (0, 0)),
    )
    out, gd, gu = pl.pallas_call(
        finish_kernel,
        grid=(grid,),
        out_shape=tuple(jax.ShapeDtypeStruct(a.shape, a.dtype) for a in (out, gd, gu)),
        in_specs=blocks,
        out_specs=blocks,
        compiler_params=pltpu.CompilerParams(vmem_limit_bytes=60 * 2**20),
    )(out, gd, gu)
    return out, gd.T[None], gu[None]


def weight_body(
    inputs,
    value_output_gradient,
    value_projection_weight,
    adapter_down_factor,
    adapter_up_factor,
    membership,
    active_token_lengths,
):
    tok_rows = inputs.shape[0]
    feat_half = inputs.shape[1]
    job_count = membership.shape[0]
    rank_dimension_size = adapter_down_factor.shape[1]
    live_rows = lax.iota(jnp.int32, tok_rows) < active_token_lengths[0]
    grad_masked = jnp.where(
        live_rows[:, None], value_output_gradient, jnp.zeros_like(value_output_gradient)
    )
    own_jobs = membership[:, 0]
    owned_weight_rows = own_jobs.astype(jnp.bfloat16)
    tenant_token_rows = lax.psum(
        own_jobs.astype(jnp.float32) * active_token_lengths[0].astype(jnp.float32), "dp"
    )
    every_down_factor = lax.all_gather(adapter_down_factor, ("dp", "tensor"), axis=2, tiled=True)
    job_down_factor = jnp.einsum(
        "j,jrd->rd", owned_weight_rows, every_down_factor, preferred_element_type=jnp.float32
    ).astype(jnp.bfloat16)
    up_job = jnp.einsum(
        "p,pxh->xh", owned_weight_rows, adapter_up_factor, preferred_element_type=jnp.float32
    ).astype(jnp.bfloat16)
    resident_down_factor = lax.dynamic_slice_in_dim(
        job_down_factor, lax.axis_index("tensor") * feat_half, feat_half, 1
    )
    down_terms = contract_cols(inputs, resident_down_factor)
    up_terms = contract_cols(grad_masked, up_job)
    projected_full, back_full = lax.psum((down_terms, up_terms), "tensor")
    projected = jnp.where(
        live_rows[:, None], projected_full, jnp.zeros_like(projected_full)
    ).astype(jnp.bfloat16)
    rank_gradient_back = back_full.astype(jnp.bfloat16)
    frozen_terms = contract_cols(
        grad_masked, lax.all_gather(value_projection_weight, "dp", axis=0, tiled=True)
    )
    fixed_weight = lax.psum_scatter(
        frozen_terms.astype(jnp.bfloat16), "tensor", scatter_dimension=1, tiled=True
    ).astype(jnp.float32)
    grad_inputs = (
        fixed_weight
        + adapter_scale
        * jnp.dot(rank_gradient_back, resident_down_factor, preferred_element_type=jnp.float32)
    ).astype(jnp.bfloat16)
    wide_cols = job_count * rank_dimension_size
    factor_column_count = jnp.repeat(adapter_scale / tenant_token_rows, rank_dimension_size)
    back_expand = (rank_gradient_back[:, None, :] * owned_weight_rows[None, :, None]).reshape(
        tok_rows, wide_cols
    )
    columns = inputs
    down_sums = lax.psum_scatter(
        contract_rows(columns, back_expand), "dp", scatter_dimension=0, tiled=True
    )
    proj_expand = (projected[:, None, :] * owned_weight_rows[None, :, None]).reshape(
        tok_rows, wide_cols
    )
    columns = grad_masked
    up_sums = lax.psum_scatter(
        contract_rows(columns, proj_expand), "dp", scatter_dimension=0, tiled=True
    )
    grad_down = (down_sums * factor_column_count[None, :])[None]
    grad_up = (up_sums * factor_column_count[None, :])[None]
    return (grad_inputs, grad_down, grad_up)


def solution(mesh):
    in_specs = (
        P(("groups", "dp"), "tensor"),
        P(("groups", "dp"), "tensor"),
        P("dp", "tensor"),
        P(None, None, ("dp", "tensor")),
        P(None, None, "tensor"),
        P(None, ("groups", "dp")),
        P(("groups", "dp")),
    )
    out_specs = (
        P(("groups", "dp"), "tensor"),
        P("tensor", ("groups", "dp"), None),
        P("tensor", ("groups", "dp"), None),
    )

    def body(*args):
        dp = mesh.shape["dp"]
        tok, heads = args[1].shape
        jobs, rank, feats = args[3].shape
        tokens_travel = (
            args[2].shape[0] > tok
            and mesh.shape["tensor"] == 2
            and dp == 8
            and args[2].shape[0] == 2 * feats
            and tok == 128
            and rank == 16
            and jobs * rank < 128
            and feats % 128 == 0
            and heads % (8 * dp) == 0
            and 128 % (heads // dp) == 0
        )
        if tokens_travel:
            return token_body(dp, *args)
        return weight_body(*args)

    return jax.shard_map(body, mesh=mesh, in_specs=in_specs, out_specs=out_specs, check_vma=False)
```

```python
import functools

import jax
import jax.numpy as jnp
from jax import lax
from jax.experimental import pallas as pl
from jax.experimental.pallas import tpu as pltpu
from jax.sharding import PartitionSpec as P

adapter_scale = 2.0
cuts = 2
MESH = pl.DeviceIdType.MESH


def contract_rows(left, right):
    return lax.dot_general(
        left, right, (((0,), (0,)), ((), ())), preferred_element_type=jnp.float32
    )


def contract_cols(left, right):
    return lax.dot_general(
        left, right, (((1,), (1,)), ((), ())), preferred_element_type=jnp.float32
    )


def plain_dot(left, right):
    return jnp.dot(left, right, preferred_element_type=jnp.float32)


def wide(row, lanes):
    return jnp.concatenate([row] * (lanes // row.shape[1]), axis=1)


def exchange_kernel(
    dp,
    jobs,
    rank,
    x_hbm,
    g_hbm,
    w_hbm,
    down_hbm,
    up_hbm,
    member_ref,
    length_ref,
    out_ref,
    gd_ref,
    gu_ref,
    x_ref, g_ref, w_ref, down_ref, up_ref,
    grads,
    w_sib,
    up_sib,
    meta,
    down_out,
    down_in,
    out_buf,
    part_out,
    part_in,
    proj_half,
    proj,
    load_s, meta_s, meta_r, g_s, g_r, f_s, zf_s, gf_s, gf_r, one_s, one_r,
    d_s, d_r, o_s, o_r, p_s, p_r, j_s, j_r,
):
    tok, heads = g_ref.shape
    feats = down_ref.shape[1]
    cols = jobs * rank
    gi, me, core = lax.axis_index("groups"), lax.axis_index("dp"), lax.axis_index("tensor")
    other = 1 - core
    depth = dp // 2
    z, x = me // 2, me % 2
    owner_core = me // depth
    slot = (2 * me + core) % dp
    ahead = [lax.rem(me + s, dp) for s in range(dp)]

    def remote(src, dst, send, recv, to_dp, to_core):
        return pltpu.make_async_remote_copy(
            src_ref=src, dst_ref=dst, send_sem=send, recv_sem=recv,
            device_id=(gi, to_dp, to_core), device_id_type=MESH,
        )

    loads = [
        pltpu.make_async_copy(src, dst, load_s.at[i])
        for i, (src, dst) in enumerate(
            [(g_hbm, g_ref), (up_hbm, up_ref), (down_hbm, down_ref), (w_hbm, w_ref), (x_hbm, x_ref)]
        )
    ]
    for load in loads:
        load.start()

    barrier = pltpu.get_barrier_semaphore()
    for s in range(dp):
        for c in range(2):
            if s == 0 and c == 1:
                continue
            to_core = other if s == 0 else c
            pl.semaphore_signal(
                barrier, inc=1, device_id=(gi, ahead[s], to_core), device_id_type=MESH
            )

    column = lax.broadcasted_iota(jnp.int32, (1, 128), 1)
    marks = (column >= cols).astype(jnp.int32) * length_ref[0]
    for j in range(jobs):
        marks = marks + (column // rank == j).astype(jnp.int32) * member_ref[j]
    meta[me] = marks
    length = jnp.zeros((1, 128), jnp.int32) + length_ref[0]
    live = lax.broadcasted_iota(jnp.int32, (tok, heads), 0) < wide(length, heads)
    loads[0].wait()
    grads[me, core] = jnp.where(live, g_ref[...], jnp.zeros_like(g_ref))
    loads[1].wait()
    pl.semaphore_wait(barrier, 2 * dp - 1)

    sent = []

    def go(copy):
        copy.start()
        sent.append(copy)

    pair, inner_far, end_far = z ^ 1, jnp.where(z < depth // 2, 2, 1), jnp.where(z < depth // 2, 3, 0)
    is_inner = jnp.logical_or(z == 1, z == 2)
    beside, paired = z * 2 + (1 - x), pair * 2 + x
    height = tok // cuts

    def cut(b, c, h):
        return grads.at[b, c, h * height:(h + 1) * height, :]

    for h in range(cuts):
        own, n = cut(me, core, h), me * cuts + h
        go(remote(own, own, gf_s.at[n], gf_r.at[n], me, other))
    go(remote(up_ref, up_sib, one_s.at[0], one_r.at[0], me, other))
    for s in range(1, dp):
        go(remote(meta.at[me], meta.at[me], meta_s.at[ahead[s]], meta_r.at[me], ahead[s], core))
    for to in (inner_far * 2 + x, paired, beside):
        for h in range(cuts):
            own = cut(me, core, h)
            go(remote(own, own, g_s.at[to * cuts + h], g_r.at[me * cuts + h], to, core))
    loads[3].wait()
    w_half = w_ref.at[pl.ds(pl.multiple_of(other * feats, feats), feats), :]
    go(remote(w_half, w_sib, one_s.at[1], one_r.at[1], me, other))

    def got(dst, recv):
        remote(dst, dst, one_s.at[0], recv, me, other).wait_recv()

    def pick(rows, held_of):
        n = rows.shape[1]
        total = jnp.zeros((rank, n), jnp.float32)
        for j in range(jobs):
            held = held_of(j)
            total = total + rows[j * rank:(j + 1) * rank, :].astype(jnp.float32) * wide(held, n)
        return total.astype(jnp.bfloat16)

    def own_held(j):
        return jnp.zeros((1, 128), jnp.float32) + member_ref[j].astype(jnp.float32)

    got(up_sib, one_r.at[0])
    for h in range(cuts):
        got(cut(me, other, h), gf_r.at[me * cuts + h])
    up_own, up_other = up_ref[...], up_sib[...]
    back = contract_cols(pick(up_own, own_held), grads[me, core]) + contract_cols(
        pick(up_other, own_held), grads[me, other]
    )
    back = back.astype(jnp.bfloat16)
    loads[4].wait()
    for b in range(dp):
        part_out[b] = plain_dot(back, x_ref[:, b * feats:(b + 1) * feats]).astype(jnp.bfloat16)
    part_in[me] = part_out[me]
    for s in range(1, dp):
        b = ahead[s]
        go(remote(part_out.at[b], part_in.at[me], p_s.at[b], p_r.at[me], b, core))
    for s in range(1, dp):
        got(meta.at[ahead[s]], meta_r.at[ahead[s]])
    all_marks = meta[...].reshape(dp, 128).astype(jnp.float32)
    lanes = lax.broadcasted_iota(jnp.int32, (dp, 128), 1)

    def spread(lane):
        one = jnp.where(lanes == lane, all_marks, jnp.zeros_like(all_marks))
        return jnp.broadcast_to(jnp.sum(one, axis=1, keepdims=True), (dp, 128))

    holds = [spread(j * rank) for j in range(jobs)]
    lengths = spread(cols)
    loads[2].wait()
    down_all = down_ref[...]
    for b in range(dp):
        down_out[b] = pick(down_all, lambda j: holds[j][b:b + 1, :])

    mine = owner_core == core

    def to_owner(src, dst, send, recv, b):
        @pl.when(jnp.logical_and(b == me, mine))
        def _():
            pltpu.make_async_copy(src, dst, recv).start()

        @pl.when(jnp.logical_not(jnp.logical_and(b == me, mine)))
        def _():
            remote(src, dst, send, recv, b, owner_core).start()

    def to_owner_done(src, dst, send, recv, b):
        @pl.when(jnp.logical_not(jnp.logical_and(b == me, mine)))
        def _():
            remote(src, dst, send, recv, b, owner_core).wait_send()

    for s in range(dp):
        b = ahead[s]
        to_owner(down_out.at[b], down_in.at[slot], d_s.at[b], d_r.at[slot], b)

    got(w_sib, one_r.at[1])
    w_own = w_ref.at[pl.ds(pl.multiple_of(core * feats, feats), feats), :]
    out_cols = pl.ds(pl.multiple_of(slot * feats, feats), feats)

    far = []

    def arrive(zs, dx, direct=False):
        b = zs * 2 + (x if dx == 0 else 1 - x)
        for h in range(cuts):
            block, n = cut(b, core, h), b * cuts + h
            got(block, g_r.at[n])
            if direct:
                copy = remote(block, block, zf_s.at[n], g_r.at[n], paired, core)
                pl.when(is_inner)(copy.start)
                far.append(copy)
            if dx == 0:
                go(remote(block, block, f_s.at[n], g_r.at[n], beside, core))
            go(remote(block, block, gf_s.at[n], gf_r.at[n], me, other))
        return b

    def block_out(b, wait_half):
        if wait_half:
            for h in range(cuts):
                got(cut(b, other, h), gf_r.at[b * cuts + h])
        g_own, g_other = grads[b, core], grads[b, other]
        frozen = contract_cols(g_own, w_own[...]) + contract_cols(g_other, w_sib[...])
        rb = contract_cols(g_own, up_own) + contract_cols(g_other, up_other)
        held = meta[b][:, :cols].astype(jnp.float32)
        rb = (rb.astype(jnp.bfloat16).astype(jnp.float32) * held).astype(jnp.bfloat16)
        out_buf[b] = (frozen + adapter_scale * plain_dot(rb, down_all)).astype(jnp.bfloat16)
        to_owner(out_buf.at[b], out_ref.at[:, out_cols], o_s.at[b], o_r.at[slot], b)

    order = [
        (inner_far, 0, True), (pair, 0), (end_far, 0, True), (z, 1),
        (inner_far, 1), (pair, 1), (end_far, 1), None,
    ]
    held_b = arrive(*order[0])
    for i in range(dp):
        later = me
        if i + 1 < dp and order[i + 1] is not None:
            later = arrive(*order[i + 1])
        block_out(held_b, order[i] is not None)
        held_b = later
        if i == depth - 1:
            total = jnp.zeros((rank, tok), jnp.float32)
            for k in range(dp):
                got(down_in.at[k], d_r.at[k])
                total = total + contract_cols(down_in[k], x_ref[:, k * feats:(k + 1) * feats])
            proj_half[core] = total
            half = proj_half.at[core]
            go(remote(half, half, one_s.at[2], one_r.at[2], me, other))
        if i == depth:
            got(proj_half.at[other], one_r.at[2])
            full = proj_half[0] + proj_half[1]
            alive = lax.broadcasted_iota(jnp.int32, (rank, tok), 1) < length
            proj[me] = jnp.where(alive, full, jnp.zeros_like(full)).astype(jnp.bfloat16)
            for s in range(1, dp):
                go(remote(proj.at[me], proj.at[me], j_s.at[ahead[s]], j_r.at[me], ahead[s], core))

    tokens = jnp.sum(all_marks * lengths, axis=0, keepdims=True)
    factor = adapter_scale / tokens[:, :cols]

    for s in range(1, dp):
        got(part_in.at[ahead[s]], p_r.at[ahead[s]])
    same = (
        lax.broadcasted_iota(jnp.int32, (rank, 128), 1) % rank
        == lax.broadcasted_iota(jnp.int32, (rank, 128), 0)
    ).astype(jnp.float32)
    place = jnp.concatenate(
        [same * all_marks[b:b + 1, :] for b in range(dp)], axis=0
    ).astype(jnp.bfloat16)
    parts = part_in[...].reshape(dp * rank, feats)
    sums = contract_rows(place, parts)
    for j in range(jobs):
        held = jnp.sum(holds[j] * lengths, axis=0, keepdims=True)
        gd_ref[j * rank:(j + 1) * rank, :] = sums[j * rank:(j + 1) * rank, :] * wide(
            adapter_scale / held, feats
        )

    up_rows = heads // dp
    first = pl.multiple_of((me * up_rows) // 128 * 128, 128)
    total = jnp.zeros((128, cols), jnp.float32)
    for s in range(1, dp):
        got(proj.at[ahead[s]], j_r.at[ahead[s]])
    for b in range(dp):
        p_b = proj[b].astype(jnp.float32)
        wide_p = jnp.concatenate(
            [p_b * holds[j][b:b + 1, :] for j in range(jobs)], axis=0
        ).astype(jnp.bfloat16)
        g_b = grads[b, core, :, pl.ds(first, 128)]
        total = total + lax.dot_general(
            g_b, wide_p, (((0,), (1,)), ((), ())), preferred_element_type=jnp.float32
        )
    total = total * factor
    picked = total[:up_rows]
    for q in range(1, 128 // up_rows):
        picked = jnp.where(me % (128 // up_rows) == q, total[q * up_rows:(q + 1) * up_rows], picked)
    gu_ref[...] = picked

    for k in range(dp):
        got(out_ref.at[:, k * feats:(k + 1) * feats], o_r.at[k])
    for s in range(dp):
        b = ahead[s]
        to_owner_done(down_out.at[b], down_in.at[slot], d_s.at[b], d_r.at[slot], b)
        to_owner_done(out_buf.at[b], out_ref.at[:, out_cols], o_s.at[b], o_r.at[slot], b)
    for copy in far:
        pl.when(is_inner)(copy.wait_send)
    for copy in sent:
        copy.wait_send()


def finish_kernel(out_in, gd_in, gu_in, out_ref, gd_ref, gu_ref):
    out_ref[...] = out_in[...]
    gd_ref[...] = gd_in[...]
    gu_ref[...] = gu_in[...]


def token_body(
    dp,
    inputs,
    value_output_gradient,
    value_projection_weight,
    adapter_down_factor,
    adapter_up_factor,
    membership,
    active_token_lengths,
):
    tok, heads = value_output_gradient.shape
    jobs, rank, feats = adapter_down_factor.shape
    cols = jobs * rank
    bf16, f32 = jnp.bfloat16, jnp.float32
    vmem = pl.BlockSpec(memory_space=pltpu.VMEM)
    hbm = pl.BlockSpec(memory_space=pltpu.HBM)
    smem = pl.BlockSpec(memory_space=pltpu.SMEM)
    dma = pltpu.SemaphoreType.DMA
    out, gd, gu = pl.pallas_call(
        functools.partial(exchange_kernel, dp, jobs, rank),
        out_shape=(
            jax.ShapeDtypeStruct((tok, dp * feats), bf16),
            jax.ShapeDtypeStruct((cols, feats), f32),
            jax.ShapeDtypeStruct((heads // dp, cols), f32),
        ),
        in_specs=[hbm] * 5 + [smem] * 2,
        out_specs=(pl.BlockSpec(memory_space=pl.ANY), vmem, vmem),
        scratch_shapes=[
            pltpu.VMEM((tok, dp * feats), bf16),
            pltpu.VMEM((tok, heads), bf16),
            pltpu.VMEM((2 * feats, heads), bf16),
            pltpu.VMEM((cols, feats), bf16),
            pltpu.VMEM((cols, heads), bf16),
            pltpu.VMEM((dp, 2, tok, heads), bf16),
            pltpu.VMEM((feats, heads), bf16),
            pltpu.VMEM((cols, heads), bf16),
            pltpu.VMEM((dp, 1, 128), jnp.int32),
            pltpu.VMEM((dp, rank, feats), bf16),
            pltpu.VMEM((dp, rank, feats), bf16),
            pltpu.VMEM((dp, tok, feats), bf16),
            pltpu.VMEM((dp, rank, feats), bf16),
            pltpu.VMEM((dp, rank, feats), bf16),
            pltpu.VMEM((2, rank, tok), f32),
            pltpu.VMEM((dp, rank, tok), bf16),
        ]
        + [dma((5,))]
        + [dma((dp,))] * 2
        + [dma((dp * cuts,))] * 6
        + [dma((3,))] * 2
        + [dma((dp,))] * 8,
        compiler_params=pltpu.CompilerParams(
            collective_id=0, has_side_effects=True, vmem_limit_bytes=60 * 2**20
        ),
        cost_estimate=pl.CostEstimate(
            flops=2 * dp * tok * 2 * heads * feats, bytes_accessed=2**23, transcendentals=0
        ),
    )(
        inputs,
        value_output_gradient,
        value_projection_weight,
        adapter_down_factor.reshape(cols, feats),
        adapter_up_factor.reshape(cols, heads),
        membership.reshape(jobs),
        active_token_lengths,
    )
    grid = 2
    blocks = (
        pl.BlockSpec((tok, dp * feats // grid), lambda i: (0, i)),
        pl.BlockSpec((cols, feats // grid), lambda i: (0, i)),
        pl.BlockSpec((heads // dp, cols), lambda i: (0, 0)),
    )
    out, gd, gu = pl.pallas_call(
        finish_kernel,
        grid=(grid,),
        out_shape=tuple(jax.ShapeDtypeStruct(a.shape, a.dtype) for a in (out, gd, gu)),
        in_specs=blocks,
        out_specs=blocks,
        compiler_params=pltpu.CompilerParams(vmem_limit_bytes=60 * 2**20),
    )(out, gd, gu)
    return out, gd.T[None], gu[None]


def weight_body(
    inputs,
    value_output_gradient,
    value_projection_weight,
    adapter_down_factor,
    adapter_up_factor,
    membership,
    active_token_lengths,
):
    tok_rows = inputs.shape[0]
    feat_half = inputs.shape[1]
    job_count = membership.shape[0]
    rank_dimension_size = adapter_down_factor.shape[1]
    live_rows = lax.iota(jnp.int32, tok_rows) < active_token_lengths[0]
    grad_masked = jnp.where(
        live_rows[:, None], value_output_gradient, jnp.zeros_like(value_output_gradient)
    )
    own_jobs = membership[:, 0]
    owned_weight_rows = own_jobs.astype(jnp.bfloat16)
    tenant_token_rows = lax.psum(
        own_jobs.astype(jnp.float32) * active_token_lengths[0].astype(jnp.float32), "dp"
    )
    every_down_factor = lax.all_gather(adapter_down_factor, ("dp", "tensor"), axis=2, tiled=True)
    job_down_factor = jnp.einsum(
        "j,jrd->rd", owned_weight_rows, every_down_factor, preferred_element_type=jnp.float32
    ).astype(jnp.bfloat16)
    up_job = jnp.einsum(
        "p,pxh->xh", owned_weight_rows, adapter_up_factor, preferred_element_type=jnp.float32
    ).astype(jnp.bfloat16)
    resident_down_factor = lax.dynamic_slice_in_dim(
        job_down_factor, lax.axis_index("tensor") * feat_half, feat_half, 1
    )
    down_terms = contract_cols(inputs, resident_down_factor)
    up_terms = contract_cols(grad_masked, up_job)
    projected_full, back_full = lax.psum((down_terms, up_terms), "tensor")
    projected = jnp.where(
        live_rows[:, None], projected_full, jnp.zeros_like(projected_full)
    ).astype(jnp.bfloat16)
    rank_gradient_back = back_full.astype(jnp.bfloat16)
    frozen_terms = contract_cols(
        grad_masked, lax.all_gather(value_projection_weight, "dp", axis=0, tiled=True)
    )
    fixed_weight = lax.psum_scatter(
        frozen_terms.astype(jnp.bfloat16), "tensor", scatter_dimension=1, tiled=True
    ).astype(jnp.float32)
    grad_inputs = (
        fixed_weight
        + adapter_scale
        * jnp.dot(rank_gradient_back, resident_down_factor, preferred_element_type=jnp.float32)
    ).astype(jnp.bfloat16)
    wide_cols = job_count * rank_dimension_size
    factor_column_count = jnp.repeat(adapter_scale / tenant_token_rows, rank_dimension_size)
    back_expand = (rank_gradient_back[:, None, :] * owned_weight_rows[None, :, None]).reshape(
        tok_rows, wide_cols
    )
    columns = inputs
    down_sums = lax.psum_scatter(
        contract_rows(columns, back_expand), "dp", scatter_dimension=0, tiled=True
    )
    proj_expand = (projected[:, None, :] * owned_weight_rows[None, :, None]).reshape(
        tok_rows, wide_cols
    )
    columns = grad_masked
    up_sums = lax.psum_scatter(
        contract_rows(columns, proj_expand), "dp", scatter_dimension=0, tiled=True
    )
    grad_down = (down_sums * factor_column_count[None, :])[None]
    grad_up = (up_sums * factor_column_count[None, :])[None]
    return (grad_inputs, grad_down, grad_up)


def solution(mesh):
    in_specs = (
        P(("groups", "dp"), "tensor"),
        P(("groups", "dp"), "tensor"),
        P("dp", "tensor"),
        P(None, None, ("dp", "tensor")),
        P(None, None, "tensor"),
        P(None, ("groups", "dp")),
        P(("groups", "dp")),
    )
    out_specs = (
        P(("groups", "dp"), "tensor"),
        P("tensor", ("groups", "dp"), None),
        P("tensor", ("groups", "dp"), None),
    )

    def body(*args):
        dp = mesh.shape["dp"]
        tok, heads = args[1].shape
        jobs, rank, feats = args[3].shape
        tokens_travel = (
            args[2].shape[0] > tok
            and mesh.shape["tensor"] == 2
            and dp == 8
            and args[2].shape[0] == 2 * feats
            and tok == 128
            and rank == 16
            and jobs * rank < 128
            and feats % 128 == 0
            and heads % (8 * dp) == 0
            and 128 % (heads // dp) == 0
        )
        if tokens_travel:
            return token_body(dp, *args)
        return weight_body(*args)

    return jax.shard_map(body, mesh=mesh, in_specs=in_specs, out_specs=out_specs, check_vma=False)
```

```python
import functools

import jax
import jax.numpy as jnp
from jax import lax
from jax.experimental import pallas as pl
from jax.experimental.pallas import tpu as pltpu
from jax.sharding import PartitionSpec as P

adapter_scale = 2.0
cuts = 2
MESH = pl.DeviceIdType.MESH


def contract_rows(left, right):
    return lax.dot_general(
        left, right, (((0,), (0,)), ((), ())), preferred_element_type=jnp.float32
    )


def contract_cols(left, right):
    return lax.dot_general(
        left, right, (((1,), (1,)), ((), ())), preferred_element_type=jnp.float32
    )


def plain_dot(left, right):
    return jnp.dot(left, right, preferred_element_type=jnp.float32)


def wide(row, lanes):
    return jnp.concatenate([row] * (lanes // row.shape[1]), axis=1)


def exchange_kernel(
    dp,
    jobs,
    rank,
    x_hbm,
    g_hbm,
    w_hbm,
    down_hbm,
    up_hbm,
    member_ref,
    length_ref,
    out_ref,
    gd_ref,
    gu_ref,
    x_ref, g_ref, w_ref, down_ref, up_ref,
    grads,
    w_sib,
    up_sib,
    meta,
    down_out,
    down_in,
    out_buf,
    part_out,
    part_in,
    proj_half,
    proj,
    load_s, meta_s, meta_r, g_s, g_r, f_s, zf_s, gf_s, gf_r, one_s, one_r,
    d_s, d_r, o_s, o_r, p_s, p_r, j_s, j_r,
):
    tok, heads = g_ref.shape
    feats = down_ref.shape[1]
    cols = jobs * rank
    gi, me, core = lax.axis_index("groups"), lax.axis_index("dp"), lax.axis_index("tensor")
    other = 1 - core
    depth = dp // 2
    z, x = me // 2, me % 2
    owner_core = me // depth
    slot = (2 * me + core) % dp
    ahead = [lax.rem(me + s, dp) for s in range(dp)]

    def remote(src, dst, send, recv, to_dp, to_core):
        return pltpu.make_async_remote_copy(
            src_ref=src, dst_ref=dst, send_sem=send, recv_sem=recv,
            device_id=(gi, to_dp, to_core), device_id_type=MESH,
        )

    loads = [
        pltpu.make_async_copy(src, dst, load_s.at[i])
        for i, (src, dst) in enumerate(
            [(g_hbm, g_ref), (up_hbm, up_ref), (down_hbm, down_ref), (w_hbm, w_ref), (x_hbm, x_ref)]
        )
    ]
    for load in loads:
        load.start()

    barrier = pltpu.get_barrier_semaphore()
    for s in range(dp):
        for c in range(2):
            if s == 0 and c == 1:
                continue
            to_core = other if s == 0 else c
            pl.semaphore_signal(
                barrier, inc=1, device_id=(gi, ahead[s], to_core), device_id_type=MESH
            )

    column = lax.broadcasted_iota(jnp.int32, (1, 128), 1)
    marks = (column >= cols).astype(jnp.int32) * length_ref[0]
    for j in range(jobs):
        marks = marks + (column // rank == j).astype(jnp.int32) * member_ref[j]
    meta[me] = marks
    length = jnp.zeros((1, 128), jnp.int32) + length_ref[0]
    live = lax.broadcasted_iota(jnp.int32, (tok, heads), 0) < wide(length, heads)
    loads[0].wait()
    grads[me, core] = jnp.where(live, g_ref[...], jnp.zeros_like(g_ref))
    loads[1].wait()
    pl.semaphore_wait(barrier, 2 * dp - 1)

    sent = []

    def go(copy):
        copy.start()
        sent.append(copy)

    pair, inner_far, end_far = z ^ 1, jnp.where(z < depth // 2, 2, 1), jnp.where(z < depth // 2, 3, 0)
    is_inner = jnp.logical_or(z == 1, z == 2)
    beside, paired = z * 2 + (1 - x), pair * 2 + x
    height = tok // cuts

    def cut(b, c, h):
        return grads.at[b, c, h * height:(h + 1) * height, :]

    for h in range(cuts):
        own, n = cut(me, core, h), me * cuts + h
        go(remote(own, own, gf_s.at[n], gf_r.at[n], me, other))
    go(remote(up_ref, up_sib, one_s.at[0], one_r.at[0], me, other))
    for s in range(1, dp):
        go(remote(meta.at[me], meta.at[me], meta_s.at[ahead[s]], meta_r.at[me], ahead[s], core))
    for to in (inner_far * 2 + x, paired, beside):
        for h in range(cuts):
            own = cut(me, core, h)
            go(remote(own, own, g_s.at[to * cuts + h], g_r.at[me * cuts + h], to, core))
    loads[3].wait()
    w_half = w_ref.at[pl.ds(pl.multiple_of(other * feats, feats), feats), :]
    go(remote(w_half, w_sib, one_s.at[1], one_r.at[1], me, other))

    def got(dst, recv):
        remote(dst, dst, one_s.at[0], recv, me, other).wait_recv()

    def pick(rows, held_of):
        n = rows.shape[1]
        total = jnp.zeros((rank, n), jnp.float32)
        for j in range(jobs):
            held = held_of(j)
            total = total + rows[j * rank:(j + 1) * rank, :].astype(jnp.float32) * wide(held, n)
        return total.astype(jnp.bfloat16)

    def own_held(j):
        return jnp.zeros((1, 128), jnp.float32) + member_ref[j].astype(jnp.float32)

    got(up_sib, one_r.at[0])
    for h in range(cuts):
        got(cut(me, other, h), gf_r.at[me * cuts + h])
    up_own, up_other = up_ref[...], up_sib[...]
    back = contract_cols(pick(up_own, own_held), grads[me, core]) + contract_cols(
        pick(up_other, own_held), grads[me, other]
    )
    back = back.astype(jnp.bfloat16)
    loads[4].wait()
    for b in range(dp):
        part_out[b] = plain_dot(back, x_ref[:, b * feats:(b + 1) * feats]).astype(jnp.bfloat16)
    part_in[me] = part_out[me]
    for s in sorted(range(1, dp), key=lambda s: abs(2 * s - dp)):
        b = ahead[s]
        go(remote(part_out.at[b], part_in.at[me], p_s.at[b], p_r.at[me], b, core))
    for s in range(1, dp):
        got(meta.at[ahead[s]], meta_r.at[ahead[s]])
    all_marks = meta[...].reshape(dp, 128).astype(jnp.float32)
    lanes = lax.broadcasted_iota(jnp.int32, (dp, 128), 1)

    def spread(lane):
        one = jnp.where(lanes == lane, all_marks, jnp.zeros_like(all_marks))
        return jnp.broadcast_to(jnp.sum(one, axis=1, keepdims=True), (dp, 128))

    holds = [spread(j * rank) for j in range(jobs)]
    lengths = spread(cols)
    loads[2].wait()
    down_all = down_ref[...]
    for b in range(dp):
        down_out[b] = pick(down_all, lambda j: holds[j][b:b + 1, :])

    mine = owner_core == core

    def to_owner(src, dst, send, recv, b):
        @pl.when(jnp.logical_and(b == me, mine))
        def _():
            pltpu.make_async_copy(src, dst, recv).start()

        @pl.when(jnp.logical_not(jnp.logical_and(b == me, mine)))
        def _():
            remote(src, dst, send, recv, b, owner_core).start()

    def to_owner_done(src, dst, send, recv, b):
        @pl.when(jnp.logical_not(jnp.logical_and(b == me, mine)))
        def _():
            remote(src, dst, send, recv, b, owner_core).wait_send()

    for s in sorted(range(dp), key=lambda s: abs(2 * s - dp)):
        b = ahead[s]
        to_owner(down_out.at[b], down_in.at[slot], d_s.at[b], d_r.at[slot], b)

    got(w_sib, one_r.at[1])
    w_own = w_ref.at[pl.ds(pl.multiple_of(core * feats, feats), feats), :]
    out_cols = pl.ds(pl.multiple_of(slot * feats, feats), feats)

    far = []

    def arrive(zs, dx, direct=False):
        b = zs * 2 + (x if dx == 0 else 1 - x)
        for h in range(cuts):
            block, n = cut(b, core, h), b * cuts + h
            got(block, g_r.at[n])
            if direct:
                copy = remote(block, block, zf_s.at[n], g_r.at[n], paired, core)
                pl.when(is_inner)(copy.start)
                far.append(copy)
            if dx == 0:
                go(remote(block, block, f_s.at[n], g_r.at[n], beside, core))
            go(remote(block, block, gf_s.at[n], gf_r.at[n], me, other))
        return b

    def block_out(b, wait_half):
        if wait_half:
            for h in range(cuts):
                got(cut(b, other, h), gf_r.at[b * cuts + h])
        g_own, g_other = grads[b, core], grads[b, other]
        frozen = contract_cols(g_own, w_own[...]) + contract_cols(g_other, w_sib[...])
        rb = contract_cols(g_own, up_own) + contract_cols(g_other, up_other)
        held = meta[b][:, :cols].astype(jnp.float32)
        rb = (rb.astype(jnp.bfloat16).astype(jnp.float32) * held).astype(jnp.bfloat16)
        out_buf[b] = (frozen + adapter_scale * plain_dot(rb, down_all)).astype(jnp.bfloat16)
        to_owner(out_buf.at[b], out_ref.at[:, out_cols], o_s.at[b], o_r.at[slot], b)

    order = [
        (inner_far, 0, True), (pair, 0), (end_far, 0, True), (z, 1),
        (inner_far, 1), (pair, 1), (end_far, 1), None,
    ]
    held_b = arrive(*order[0])
    for i in range(dp):
        later = me
        if i + 1 < dp and order[i + 1] is not None:
            later = arrive(*order[i + 1])
        block_out(held_b, order[i] is not None)
        held_b = later
        if i == depth - 1:
            total = jnp.zeros((rank, tok), jnp.float32)
            for k in range(dp):
                got(down_in.at[k], d_r.at[k])
                total = total + contract_cols(down_in[k], x_ref[:, k * feats:(k + 1) * feats])
            proj_half[core] = total
            half = proj_half.at[core]
            go(remote(half, half, one_s.at[2], one_r.at[2], me, other))
        if i == depth:
            got(proj_half.at[other], one_r.at[2])
            full = proj_half[0] + proj_half[1]
            alive = lax.broadcasted_iota(jnp.int32, (rank, tok), 1) < length
            proj[me] = jnp.where(alive, full, jnp.zeros_like(full)).astype(jnp.bfloat16)
            for s in range(1, dp):
                go(remote(proj.at[me], proj.at[me], j_s.at[ahead[s]], j_r.at[me], ahead[s], core))

    tokens = jnp.sum(all_marks * lengths, axis=0, keepdims=True)
    factor = adapter_scale / tokens[:, :cols]

    for s in range(1, dp):
        got(part_in.at[ahead[s]], p_r.at[ahead[s]])
    same = (
        lax.broadcasted_iota(jnp.int32, (rank, 128), 1) % rank
        == lax.broadcasted_iota(jnp.int32, (rank, 128), 0)
    ).astype(jnp.float32)
    place = jnp.concatenate(
        [same * all_marks[b:b + 1, :] for b in range(dp)], axis=0
    ).astype(jnp.bfloat16)
    parts = part_in[...].reshape(dp * rank, feats)
    sums = contract_rows(place, parts)
    for j in range(jobs):
        held = jnp.sum(holds[j] * lengths, axis=0, keepdims=True)
        gd_ref[j * rank:(j + 1) * rank, :] = sums[j * rank:(j + 1) * rank, :] * wide(
            adapter_scale / held, feats
        )

    up_rows = heads // dp
    first = pl.multiple_of((me * up_rows) // 128 * 128, 128)
    total = jnp.zeros((128, cols), jnp.float32)
    for s in range(1, dp):
        got(proj.at[ahead[s]], j_r.at[ahead[s]])
    for b in range(dp):
        p_b = proj[b].astype(jnp.float32)
        wide_p = jnp.concatenate(
            [p_b * holds[j][b:b + 1, :] for j in range(jobs)], axis=0
        ).astype(jnp.bfloat16)
        g_b = grads[b, core, :, pl.ds(first, 128)]
        total = total + lax.dot_general(
            g_b, wide_p, (((0,), (1,)), ((), ())), preferred_element_type=jnp.float32
        )
    total = total * factor
    picked = total[:up_rows]
    for q in range(1, 128 // up_rows):
        picked = jnp.where(me % (128 // up_rows) == q, total[q * up_rows:(q + 1) * up_rows], picked)
    gu_ref[...] = picked

    for k in range(dp):
        got(out_ref.at[:, k * feats:(k + 1) * feats], o_r.at[k])
    for s in range(dp):
        b = ahead[s]
        to_owner_done(down_out.at[b], down_in.at[slot], d_s.at[b], d_r.at[slot], b)
        to_owner_done(out_buf.at[b], out_ref.at[:, out_cols], o_s.at[b], o_r.at[slot], b)
    for copy in far:
        pl.when(is_inner)(copy.wait_send)
    for copy in sent:
        copy.wait_send()


def finish_kernel(out_in, gd_in, gu_in, out_ref, gd_ref, gu_ref):
    out_ref[...] = out_in[...]
    gd_ref[...] = gd_in[...]
    gu_ref[...] = gu_in[...]


def token_body(
    dp,
    inputs,
    value_output_gradient,
    value_projection_weight,
    adapter_down_factor,
    adapter_up_factor,
    membership,
    active_token_lengths,
):
    tok, heads = value_output_gradient.shape
    jobs, rank, feats = adapter_down_factor.shape
    cols = jobs * rank
    bf16, f32 = jnp.bfloat16, jnp.float32
    vmem = pl.BlockSpec(memory_space=pltpu.VMEM)
    hbm = pl.BlockSpec(memory_space=pltpu.HBM)
    smem = pl.BlockSpec(memory_space=pltpu.SMEM)
    dma = pltpu.SemaphoreType.DMA
    out, gd, gu = pl.pallas_call(
        functools.partial(exchange_kernel, dp, jobs, rank),
        out_shape=(
            jax.ShapeDtypeStruct((tok, dp * feats), bf16),
            jax.ShapeDtypeStruct((cols, feats), f32),
            jax.ShapeDtypeStruct((heads // dp, cols), f32),
        ),
        in_specs=[hbm] * 5 + [smem] * 2,
        out_specs=(pl.BlockSpec(memory_space=pl.ANY), vmem, vmem),
        scratch_shapes=[
            pltpu.VMEM((tok, dp * feats), bf16),
            pltpu.VMEM((tok, heads), bf16),
            pltpu.VMEM((2 * feats, heads), bf16),
            pltpu.VMEM((cols, feats), bf16),
            pltpu.VMEM((cols, heads), bf16),
            pltpu.VMEM((dp, 2, tok, heads), bf16),
            pltpu.VMEM((feats, heads), bf16),
            pltpu.VMEM((cols, heads), bf16),
            pltpu.VMEM((dp, 1, 128), jnp.int32),
            pltpu.VMEM((dp, rank, feats), bf16),
            pltpu.VMEM((dp, rank, feats), bf16),
            pltpu.VMEM((dp, tok, feats), bf16),
            pltpu.VMEM((dp, rank, feats), bf16),
            pltpu.VMEM((dp, rank, feats), bf16),
            pltpu.VMEM((2, rank, tok), f32),
            pltpu.VMEM((dp, rank, tok), bf16),
        ]
        + [dma((5,))]
        + [dma((dp,))] * 2
        + [dma((dp * cuts,))] * 6
        + [dma((3,))] * 2
        + [dma((dp,))] * 8,
        compiler_params=pltpu.CompilerParams(
            collective_id=0, has_side_effects=True, vmem_limit_bytes=60 * 2**20
        ),
        cost_estimate=pl.CostEstimate(
            flops=2 * dp * tok * 2 * heads * feats, bytes_accessed=2**23, transcendentals=0
        ),
    )(
        inputs,
        value_output_gradient,
        value_projection_weight,
        adapter_down_factor.reshape(cols, feats),
        adapter_up_factor.reshape(cols, heads),
        membership.reshape(jobs),
        active_token_lengths,
    )
    grid = 2
    blocks = (
        pl.BlockSpec((tok, dp * feats // grid), lambda i: (0, i)),
        pl.BlockSpec((cols, feats // grid), lambda i: (0, i)),
        pl.BlockSpec((heads // dp, cols), lambda i: (0, 0)),
    )
    out, gd, gu = pl.pallas_call(
        finish_kernel,
        grid=(grid,),
        out_shape=tuple(jax.ShapeDtypeStruct(a.shape, a.dtype) for a in (out, gd, gu)),
        in_specs=blocks,
        out_specs=blocks,
        compiler_params=pltpu.CompilerParams(vmem_limit_bytes=60 * 2**20),
    )(out, gd, gu)
    return out, gd.T[None], gu[None]


def weight_body(
    inputs,
    value_output_gradient,
    value_projection_weight,
    adapter_down_factor,
    adapter_up_factor,
    membership,
    active_token_lengths,
):
    tok_rows = inputs.shape[0]
    feat_half = inputs.shape[1]
    job_count = membership.shape[0]
    rank_dimension_size = adapter_down_factor.shape[1]
    live_rows = lax.iota(jnp.int32, tok_rows) < active_token_lengths[0]
    grad_masked = jnp.where(
        live_rows[:, None], value_output_gradient, jnp.zeros_like(value_output_gradient)
    )
    own_jobs = membership[:, 0]
    owned_weight_rows = own_jobs.astype(jnp.bfloat16)
    tenant_token_rows = lax.psum(
        own_jobs.astype(jnp.float32) * active_token_lengths[0].astype(jnp.float32), "dp"
    )
    every_down_factor = lax.all_gather(adapter_down_factor, ("dp", "tensor"), axis=2, tiled=True)
    job_down_factor = jnp.einsum(
        "j,jrd->rd", owned_weight_rows, every_down_factor, preferred_element_type=jnp.float32
    ).astype(jnp.bfloat16)
    up_job = jnp.einsum(
        "p,pxh->xh", owned_weight_rows, adapter_up_factor, preferred_element_type=jnp.float32
    ).astype(jnp.bfloat16)
    resident_down_factor = lax.dynamic_slice_in_dim(
        job_down_factor, lax.axis_index("tensor") * feat_half, feat_half, 1
    )
    down_terms = contract_cols(inputs, resident_down_factor)
    up_terms = contract_cols(grad_masked, up_job)
    projected_full, back_full = lax.psum((down_terms, up_terms), "tensor")
    projected = jnp.where(
        live_rows[:, None], projected_full, jnp.zeros_like(projected_full)
    ).astype(jnp.bfloat16)
    rank_gradient_back = back_full.astype(jnp.bfloat16)
    frozen_terms = contract_cols(
        grad_masked, lax.all_gather(value_projection_weight, "dp", axis=0, tiled=True)
    )
    fixed_weight = lax.psum_scatter(
        frozen_terms.astype(jnp.bfloat16), "tensor", scatter_dimension=1, tiled=True
    ).astype(jnp.float32)
    grad_inputs = (
        fixed_weight
        + adapter_scale
        * jnp.dot(rank_gradient_back, resident_down_factor, preferred_element_type=jnp.float32)
    ).astype(jnp.bfloat16)
    wide_cols = job_count * rank_dimension_size
    factor_column_count = jnp.repeat(adapter_scale / tenant_token_rows, rank_dimension_size)
    back_expand = (rank_gradient_back[:, None, :] * owned_weight_rows[None, :, None]).reshape(
        tok_rows, wide_cols
    )
    columns = inputs
    down_sums = lax.psum_scatter(
        contract_rows(columns, back_expand), "dp", scatter_dimension=0, tiled=True
    )
    proj_expand = (projected[:, None, :] * owned_weight_rows[None, :, None]).reshape(
        tok_rows, wide_cols
    )
    columns = grad_masked
    up_sums = lax.psum_scatter(
        contract_rows(columns, proj_expand), "dp", scatter_dimension=0, tiled=True
    )
    grad_down = (down_sums * factor_column_count[None, :])[None]
    grad_up = (up_sums * factor_column_count[None, :])[None]
    return (grad_inputs, grad_down, grad_up)


def solution(mesh):
    in_specs = (
        P(("groups", "dp"), "tensor"),
        P(("groups", "dp"), "tensor"),
        P("dp", "tensor"),
        P(None, None, ("dp", "tensor")),
        P(None, None, "tensor"),
        P(None, ("groups", "dp")),
        P(("groups", "dp")),
    )
    out_specs = (
        P(("groups", "dp"), "tensor"),
        P("tensor", ("groups", "dp"), None),
        P("tensor", ("groups", "dp"), None),
    )

    def body(*args):
        dp = mesh.shape["dp"]
        tok, heads = args[1].shape
        jobs, rank, feats = args[3].shape
        tokens_travel = (
            args[2].shape[0] > tok
            and mesh.shape["tensor"] == 2
            and dp == 8
            and args[2].shape[0] == 2 * feats
            and tok == 128
            and rank == 16
            and jobs * rank < 128
            and feats % 128 == 0
            and heads % (8 * dp) == 0
            and 128 % (heads // dp) == 0
        )
        if tokens_travel:
            return token_body(dp, *args)
        return weight_body(*args)

    return jax.shard_map(body, mesh=mesh, in_specs=in_specs, out_specs=out_specs, check_vma=False)
```
